32 devices in a mesh: section: 4 (over y, core), expert: 8 (over z, x).
Axes of the slice: x: 2, y: 2, z: 4, core: 2. Of those that a mesh axis runs over, the one named last changes fastest.
Arguments:
- pending: bfloat16 [2, 4, 512, 3584], P(None, 'section', 'expert'), may hold values from -6 to 6
- routes: int32 [2, 4, 512, 1], P(None, 'section', 'expert'), may hold values from 0 to 3; in each aligned block of 64 rows (0 to 63, 64 to 127, ..., all dimensions but the last counted through in order) at most 16 rows name the same one
- probs: bfloat16 [2, 4, 512], P(None, 'section', 'expert'), may hold values from 0.049804688 to 0.94921875
- saved_gate: bfloat16 [2, 4, 8, 8, 16, 128], P(None, 'section', 'expert'), may hold values from -6 to 6
- saved_up: bfloat16 [2, 4, 8, 8, 16, 128], P(None, 'section', 'expert'), may hold values from -6 to 6
- w_gate: bfloat16 [4, 3584, 1024], P('section', None, 'expert'), may hold values from -0.09375 to 0.09375
- w_up: bfloat16 [4, 3584, 1024], P('section', None, 'expert'), may hold values from -0.09375 to 0.09375
- w_down: bfloat16 [4, 1024, 3584], P('section', 'expert'), may hold values from -0.09375 to 0.09375
- w_router: float32 [4, 3584, 4], P('section'), may hold values from -0.2 to 0.2
Outputs:
- passed: bfloat16 [2, 4, 512, 3584], P(None, 'section', 'expert')
The draws below stay inside these ranges and needn't reach their ends.
Inputs may be any that keep to these rules, and one draw needn't show every extreme that they name: `routes`: among the 64 tokens of one device, at one section and direction, each expert is chosen by exactly 16 tokens.
All inputs are finite; a program needn't handle non-finite values.
Results may differ from the reference program's by a relative error of at most 0.0031.
Values may be sent and summed in bfloat16 or wider, within the bound.
A program may use at most 64 MiB of HBM per device.

```python
import math
import jax
import jax.numpy as jnp
import numpy as np
from jax import lax

D = 3584
HS = 128
EXP_FLIGHT = 4
TOK_DEV = 64
H = 256
CAP = 16
SECTIONS = 4
TOKENS = 512
N_EXPERT = 8


def block_levels(stream_key, dims, cuts, low, top_value):
    def one(position, blocks):
        steps = jax.random.uniform(jax.random.fold_in(jax.random.fold_in(stream_key, 6), position), (blocks,), jnp.float32, low / len(cuts), top_value / len(cuts))
        return jnp.repeat(jnp.exp(steps), dims[position] // blocks).reshape((-1,) + (1,) * (len(dims) - position - 1))

    gain = one(*cuts[0])
    for cut in cuts[1:]:
        gain = gain * one(*cut)
    return gain


def routed_block(stream_key, own, number, rows, amount, top, most, lean):
    order = jax.random.permutation(stream_key, amount)
    heavy_load, common = portions_of(amount, rows * top, most, lean, True), portions_of(amount, rows * top, most, lean, False)
    places = jnp.arange(amount)

    def named(lengths, turn):
        used = int((lengths > 0).sum())
        fixed = max(1, used // 4)
        shifted = fixed + (places - fixed + turn * (used - fixed)) % max(1, amount - fixed)
        return jnp.zeros((amount,), jnp.int32).at[order[jnp.where(places < fixed, places, shifted)]].set(jnp.asarray(lengths, jnp.int32))

    lengths = jnp.where(number % 4 == 0, named(heavy_load, number // 4), named(common, number - number // 4 - 1))
    mixed = jax.random.permutation(jax.random.fold_in(own, 3), amount)
    giver, receiver = mixed[0:amount // 2 * 2:2], mixed[1:amount // 2 * 2:2]
    slack = jnp.minimum(lengths[giver] - 1, most - lengths[receiver]) // 2
    slack = jnp.where((giver == order[0]) | (receiver == order[0]) | (lengths[receiver] == 0), 0, jnp.maximum(slack, 0))
    shifted = jax.random.randint(jax.random.fold_in(own, 4), (amount // 2,), 0, 1 << 20) % (slack + 1)
    lengths = lengths.at[giver].add(-shifted).at[receiver].add(shifted)
    members = jnp.searchsorted(jnp.cumsum(lengths), jnp.arange(rows * top), side="right").astype(jnp.int32)
    table = members.reshape(top, rows).T
    table = table[jax.random.permutation(jax.random.fold_in(own, 1), rows)]
    turn = jax.random.randint(jax.random.fold_in(own, 2), (rows, 1), 0, top)
    return jnp.take_along_axis(table, (jnp.arange(top)[None, :] + turn) % top, axis=1)


def portions_of(number_of, total, bound, lean, full):
    portions = [(1 << 20) // math.isqrt(standing ** lean) + 1 for standing in range(1, number_of + 1)]
    largest = bound if full else min(bound, max(-(-total // number_of), total * portions[0] // sum(portions)))
    least = 1 if total - largest >= number_of - 1 else 0
    given, surplus = [largest] + [least] * (number_of - 1), total - largest - least * (number_of - 1)
    while surplus > 0:
        free = [i for i in range(1, number_of) if given[i] < largest] or [i for i in range(1, number_of) if given[i] < bound]
        pool, budget = sum([portions[i] for i in free]), surplus
        for i in free:
            addition = min(bound - given[i], max(1, budget * portions[i] // pool), surplus)
            given[i] = given[i] + addition
            surplus = surplus - addition
    return np.array(given)


def centred(own_key, shape, width, bound, pieces=(), kind=jnp.bfloat16):
    result = jax.random.normal(own_key, shape, jnp.float32) * width
    if len(pieces) > 0:
        result = block_levels(own_key, shape, pieces, -0.22, 0.18) * result
    return jnp.clip(result, min=-bound, max=bound).astype(kind)


def setup_inputs(seed: int = 0) -> dict:
    arg_keys = jax.random.split(jax.random.key(seed), 10)
    pending = centred(arg_keys[0], (2, SECTIONS, TOKENS, D), 1.0, 6.0, ((1, 4), (2, 8)))
    routes_keys = jax.random.split(jax.random.fold_in(arg_keys[1], 1), 2 * SECTIONS * TOKENS // TOK_DEV)
    routes_turns = jax.random.permutation(jax.random.fold_in(arg_keys[1], 3), 2 * SECTIONS * TOKENS // TOK_DEV)
    routes = jax.vmap(lambda own, number: routed_block(jax.random.fold_in(arg_keys[1], 2), own, number, TOK_DEV, EXP_FLIGHT, 1, CAP, 0))(routes_keys, routes_turns).reshape((2, SECTIONS, TOKENS, 1))
    probs = jnp.clip(0.049804688 + 0.89941406 * jax.random.uniform(arg_keys[2], (2, SECTIONS, TOKENS), jnp.float32) ** block_levels(arg_keys[2], (2, SECTIONS, TOKENS), ((1, 4), (2, 8)), -0.2, 0.2), 0.049804688, 0.94921875).astype(jnp.bfloat16)
    saved_gate = centred(arg_keys[3], (2, SECTIONS, N_EXPERT, N_EXPERT, CAP, HS), 1.5, 6.0, ((1, 4), (2, 8)))
    saved_up = centred(arg_keys[4], (2, SECTIONS, N_EXPERT, N_EXPERT, CAP, HS), 1.0, 6.0, ((1, 4), (2, 8)))
    w_gate = centred(arg_keys[5], (SECTIONS, D, EXP_FLIGHT * H), D ** -0.5, 0.09375, ((0, 4), (2, 8)))
    w_up = centred(arg_keys[6], (SECTIONS, D, EXP_FLIGHT * H), D ** -0.5, 0.09375, ((0, 4), (2, 8)))
    w_down = centred(arg_keys[7], (SECTIONS, EXP_FLIGHT * H, D), D ** -0.5, 0.09375, ((0, 4), (1, 8)))
    w_router = centred(arg_keys[8], (SECTIONS, D, EXP_FLIGHT), 0.03, 0.2, ((0, 4),), jnp.float32)
    return {"pending": pending, "routes": routes, "probs": probs, "saved_gate": saved_gate, "saved_up": saved_up, "w_gate": w_gate, "w_up": w_up, "w_down": w_down, "w_router": w_router}


def expert_rows(packed):
    rows, gate_pre, up_pre, prob, wg_e, wu_e, wd_e = packed
    grad_z = jnp.einsum('md,jkd->mjk', rows.astype(jnp.float32), wd_e.astype(jnp.float32))
    sig = jax.nn.sigmoid(gate_pre)
    hidden = gate_pre * sig * up_pre
    dots = jnp.sum(hidden * grad_z, axis=2).astype(jnp.bfloat16)
    dots = lax.optimization_barrier(dots).astype(jnp.float32)
    grad_h = prob[:, None, None] * grad_z
    grad_gate = (grad_h * up_pre * sig * (1.0 + gate_pre * (1.0 - sig))).astype(jnp.bfloat16)
    grad_up = (grad_h * gate_pre * sig).astype(jnp.bfloat16)
    parts = jnp.einsum('mjk,djk->mjd', grad_gate.astype(jnp.float32), wg_e.astype(jnp.float32))
    parts = parts + jnp.einsum('mjk,djk->mjd', grad_up.astype(jnp.float32), wu_e.astype(jnp.float32))
    parts = lax.optimization_barrier(parts.astype(jnp.bfloat16)).astype(jnp.float32)
    return jnp.sum(parts, axis=1), jnp.sum(dots, axis=1)


def layer_back(grad_in, expert_ids, prob, gate_saved, up_saved, wg, wu, wd, wr):
    group = N_EXPERT // EXP_FLIGHT
    per_dev = expert_ids.reshape(N_EXPERT, TOK_DEV)
    onehot = (per_dev[:, :, None] == jnp.arange(EXP_FLIGHT, dtype=jnp.int32)[None, None, :]).astype(jnp.int32)
    slot_index = jnp.sum((jnp.cumsum(onehot, axis=1) - 1) * onehot, axis=2).reshape(TOKENS).astype(jnp.int32)
    source = (jnp.arange(TOKENS, dtype=jnp.int32) // TOK_DEV).astype(jnp.int32)
    gate_r = gate_saved.reshape(EXP_FLIGHT, group, N_EXPERT, CAP, HS)
    up_r = up_saved.reshape(EXP_FLIGHT, group, N_EXPERT, CAP, HS)
    gate_tok = gate_r[expert_ids, :, source, slot_index, :].astype(jnp.float32)
    up_tok = up_r[expert_ids, :, source, slot_index, :].astype(jnp.float32)
    order = jnp.argsort(expert_ids, stable=True).astype(jnp.int32)
    count = TOKENS // EXP_FLIGHT
    prob_f = prob.astype(jnp.float32)
    packed = (grad_in[order].reshape(EXP_FLIGHT, count, D),
              gate_tok[order].reshape(EXP_FLIGHT, count, group, HS),
              up_tok[order].reshape(EXP_FLIGHT, count, group, HS),
              prob_f[order].reshape(EXP_FLIGHT, count),
              jnp.transpose(wg.reshape(D, EXP_FLIGHT, group, HS), (1, 0, 2, 3)),
              jnp.transpose(wu.reshape(D, EXP_FLIGHT, group, HS), (1, 0, 2, 3)),
              wd.reshape(EXP_FLIGHT, group, HS, D))
    back_sorted, dot_sorted = lax.map(expert_rows, packed)
    inverse = jnp.argsort(order).astype(jnp.int32)
    back = back_sorted.reshape(TOKENS, D)[inverse]
    dotsum = dot_sorted.reshape(TOKENS)[inverse]
    scaled = dotsum * prob_f * (1.0 - prob_f)
    router_term = scaled[:, None] * jnp.transpose(wr)[expert_ids]
    return (grad_in.astype(jnp.float32) + back + router_term).astype(jnp.bfloat16)


def reference(pending, routes, probs, saved_gate, saved_up, w_gate, w_up, w_down, w_router):
    results = []
    for direction in range(2):
        section_out = []
        for section in range(SECTIONS):
            if direction == 0:
                anchor = (section + 1) % SECTIONS
            else:
                anchor = (section - 1) % SECTIONS
            section_out.append(layer_back(pending[direction, anchor], routes[direction, section, :, 0],
                                        probs[direction, section], saved_gate[direction, section],
                                        saved_up[direction, section], w_gate[section], w_up[section],
                                        w_down[section], w_router[section]))
        results.append(jnp.stack(section_out))
    return jnp.stack(results)
```

```python
import functools

import jax
import jax.numpy as jnp
from jax import lax
from jax.experimental import pallas as pl
from jax.experimental.pallas import tpu as pltpu
from jax.sharding import PartitionSpec as P

MESH = pl.DeviceIdType.MESH
F32 = jnp.float32
BF16 = jnp.bfloat16
CHUNKS = 2


def dot(a, b, contract):
    return lax.dot_general(a, b, (contract, ((), ())), preferred_element_type=F32)


def layer_kernel(
    sections, experts, group, chunks,
    pend, routes, probs, gate, up, w_gate, w_up, w_down, router, out,
    grad, wgu, wd, picked, rows, p_own, p_got, parts, halves, sums, home,
    load_sem, shift_send, shift_recv, p_send, p_recv, there_send, there_recv,
    fwd_send, fwd_recv, red_send, red_recv, back_send, back_recv,
):
    members = experts * group
    tokens, width = grad.shape[1], grad.shape[2]
    cap = tokens // experts
    step = width // chunks
    cols = [pl.ds(c * step, step) for c in range(chunks)]
    sec, me = lax.axis_index("section"), lax.axis_index("expert")
    mine, side = me // group, me % group
    odd = sec % 2
    way = (odd, 1 - odd)
    source = (sec + 1 - 2 * odd, lax.rem(sec + sections - 1 + 2 * odd, sections))

    def at(expert, member):
        return (sec, expert * group + member)

    def remote(src, dst, send, recv, device):
        return pltpu.make_async_remote_copy(
            src_ref=src, dst_ref=dst, send_sem=send, recv_sem=recv,
            device_id=device, device_id_type=MESH)

    loads = [
        pltpu.make_async_copy(w_down, wd, load_sem.at[0]),
        pltpu.make_async_copy(w_gate, wgu.at[:, pl.ds(0, w_gate.shape[1])], load_sem.at[1]),
        pltpu.make_async_copy(
            w_up, wgu.at[:, pl.ds(w_gate.shape[1], w_up.shape[1])], load_sem.at[2]),
    ]
    for load in loads:
        load.start()

    barrier = pltpu.get_barrier_semaphore()
    for other in source:
        pl.semaphore_signal(barrier, inc=1, device_id=(other, me), device_id_type=MESH)
    for k in range(1, members):
        pl.semaphore_signal(
            barrier, inc=1, device_id=(sec, lax.rem(me + k, members)), device_id_type=MESH)
    pl.semaphore_wait(barrier, members + 1)

    sent = []

    def shift(f, c):
        return remote(pend.at[1 - way[f], :, cols[c]], grad.at[f, :, cols[c]],
                      shift_send.at[f, c], shift_recv.at[f, c], (source[f], me))

    for f in range(2):
        for c in range(chunks):
            copy = shift(f, c)
            copy.start()
            sent.append(copy)

    table = []
    both_routes, both_probs = routes[...], probs[...].astype(F32)
    before = (lax.broadcasted_iota(jnp.int32, (tokens, tokens), 0)
              < lax.broadcasted_iota(jnp.int32, (tokens, tokens), 1)).astype(F32)
    for f in range(2):
        swap = odd == 1
        first, second = (0, 1) if f == 0 else (1, 0)
        r = jnp.where(swap, both_routes[second:second + 1], both_routes[first:first + 1])
        p = jnp.where(swap, both_probs[second:second + 1], both_probs[first:first + 1])
        named = (lax.broadcasted_iota(jnp.int32, (8, tokens), 0) == r).astype(F32)
        count = dot(named, before, ((1,), (0,)))
        slot = jnp.sum(named * count, axis=0, keepdims=True)
        dest = r.astype(F32) * cap + slot
        select = lax.broadcasted_iota(jnp.int32, (tokens, tokens), 0).astype(F32) == dest
        table.append(select.astype(F32).astype(BF16))
        p_slot = jnp.sum(jnp.where(select, p, 0.0), axis=1, keepdims=True)
        p_own[:, f] = jnp.broadcast_to(p_slot, (tokens, 128)).astype(BF16).reshape(
            experts, cap, 128)

    def p_copy(k):
        to = lax.rem(me + k, members)
        return remote(p_own.at[to // group], p_got.at[me], p_send.at[k], p_recv.at[k], (sec, to))

    p_got[me] = p_own[mine]
    for k in range(1, members):
        copy = p_copy(k)
        copy.start()
        sent.append(copy)

    def there(f, c, k):
        to = lax.rem(mine + k, experts)
        return remote(picked.at[f, to, :, cols[c]], rows.at[f, mine, side, :, cols[c]],
                      there_send.at[f, c, k], there_recv.at[f, c, k], at(to, side))

    def forward(f, c, k, m):
        band = lax.rem(mine + experts - k, experts)
        src = picked.at[f, mine, :, cols[c]] if k == 0 else rows.at[f, band, side, :, cols[c]]
        return remote(src, rows.at[f, band, side, :, cols[c]],
                      fwd_send.at[f, c, k, m], fwd_recv.at[f, c, k, m],
                      at(mine, lax.rem(side + m, group)))

    def reduce(f, c, m):
        to = lax.rem(side + m, group)
        return remote(parts.at[f, :, to, :, cols[c]], halves.at[f, m - 1, :, :, cols[c]],
                      red_send.at[f, c, m], red_recv.at[f, c, m], at(mine, to))

    def back(f, c, k):
        to = lax.rem(mine + k, experts)
        return remote(sums.at[f, to, :, cols[c]], home.at[f, mine, :, cols[c]],
                      back_send.at[f, c, k], back_recv.at[f, c, k], at(to, side))

    def start(copy):
        copy.start()
        sent.append(copy)

    def pick(f, c):
        shift(f, c).wait_recv()
        got = dot(table[f], grad[f, :, cols[c]], ((1,), (0,))).astype(BF16)
        picked[f, :, :, cols[c]] = got.reshape(experts, cap, step)
        for k in range(experts - 1, 0, -1):
            start(there(f, c, k))
        for m in range(1, group):
            start(forward(f, c, 0, m))
        rows[f, mine, side, :, cols[c]] = picked[f, mine, :, cols[c]]

    def pass_on(f, c):
        for k in range(1, experts):
            there(f, c, k).wait_recv()
            for m in range(1, group):
                start(forward(f, c, k, m))

    def middle(f):
        z = jnp.zeros((members * cap, wd.shape[0]), F32)
        for c in range(chunks):
            for k in range(experts):
                for m in range(1, group):
                    forward(f, c, k, m).wait_recv()
            held = rows[f, :, :, :, cols[c]].reshape(members * cap, step)
            z = z + dot(held, wd[:, cols[c]], ((1,), (1,)))
        a = gate[way[f]].reshape(members * cap, -1).astype(F32)
        b = up[way[f]].reshape(members * cap, -1).astype(F32)
        p = p_got[:, f].reshape(members * cap, 128)[:, 0:1].astype(F32)
        sg = jax.nn.sigmoid(a)
        product = jnp.sum(a * sg * b * z, axis=1, keepdims=True).astype(BF16).astype(F32)
        u = p * z
        grad_gate = (u * b * sg * (1.0 + a * (1.0 - sg))).astype(BF16)
        grad_up = (u * a * sg).astype(BF16)
        hidden = jnp.concatenate([grad_gate, grad_up], axis=1)
        scaled = product * p * (1.0 - p)
        for c in range(chunks):
            column = router[pl.ds(mine, 1), cols[c]]
            part = dot(hidden, wgu[cols[c], :], ((1,), (1,))) + scaled * column
            parts[f, :, :, :, cols[c]] = part.astype(BF16).reshape(experts, group, cap, step)
            for m in range(1, group):
                start(reduce(f, c, m))

    def add_up(f, c):
        total = parts[f, :, side, :, cols[c]].astype(F32)
        for m in range(1, group):
            reduce(f, c, m).wait_recv()
            total = total + halves[f, m - 1, :, :, cols[c]].astype(F32)
        sums[f, :, :, cols[c]] = total.astype(BF16)
        for k in range(experts - 1, 0, -1):
            start(back(f, c, k))
        home[f, mine, :, cols[c]] = sums[f, mine, :, cols[c]]

    def finish(f, c):
        for k in range(1, experts):
            back(f, c, k).wait_recv()
        got = dot(table[f], home[f, :, :, cols[c]].reshape(tokens, step), ((0,), (0,)))
        out[way[f], :, cols[c]] = (grad[f, :, cols[c]].astype(F32) + got).astype(BF16)

    for c in range(chunks):
        pick(0, c)
    for c in range(chunks):
        pass_on(0, c)
        pick(1, c)
    for load in loads:
        load.wait()
    for k in range(1, members):
        p_copy(k).wait_recv()
    middle(0)
    for c in range(chunks):
        pass_on(1, c)
    for c in range(chunks):
        add_up(0, c)
    middle(1)
    for c in range(chunks):
        add_up(1, c)
    for f in range(2):
        for c in range(chunks):
            finish(f, c)
    for copy in sent:
        copy.wait_send()


def per_device(pending, routes, probs, saved_gate, saved_up, w_gate, w_up, w_down, w_router):
    sections, members = lax.axis_size("section"), lax.axis_size("expert")
    experts = w_router.shape[2]
    group = members // experts
    tokens, width = pending.shape[2], pending.shape[3]
    cap = tokens // experts
    hidden = w_gate.shape[2]
    chunks = CHUNKS
    dma, vmem = pltpu.SemaphoreType.DMA, pltpu.VMEM
    any_spec = pl.BlockSpec(memory_space=pl.ANY)
    vmem_spec = pl.BlockSpec(memory_space=pltpu.VMEM)
    result = pl.pallas_call(
        functools.partial(layer_kernel, sections, experts, group, chunks),
        out_shape=jax.ShapeDtypeStruct((2, tokens, width), BF16),
        in_specs=[any_spec] + [vmem_spec] * 4 + [any_spec] * 3 + [vmem_spec],
        out_specs=vmem_spec,
        scratch_shapes=[
            vmem((2, tokens, width), BF16),
            vmem((width, 2 * hidden), BF16),
            vmem((hidden, width), BF16),
            vmem((2, experts, cap, width), BF16),
            vmem((2, experts, group, cap, width), BF16),
            vmem((experts, 2, cap, 128), BF16),
            vmem((members, 2, cap, 128), BF16),
            vmem((2, experts, group, cap, width), BF16),
            vmem((2, max(group - 1, 1), experts, cap, width), BF16),
            vmem((2, experts, cap, width), BF16),
            vmem((2, experts, cap, width), BF16),
            dma((3,)),
            dma((2, chunks)), dma((2, chunks)),
            dma((members,)), dma((members,)),
            dma((2, chunks, experts)), dma((2, chunks, experts)),
            dma((2, chunks, experts, group)), dma((2, chunks, experts, group)),
            dma((2, chunks, group)), dma((2, chunks, group)),
            dma((2, chunks, experts)), dma((2, chunks, experts)),
        ],
        compiler_params=pltpu.CompilerParams(
            collective_id=0, has_side_effects=True, vmem_limit_bytes=56 << 20),
        cost_estimate=pl.CostEstimate(
            flops=12 * members * cap * hidden * width, bytes_accessed=8 << 20, transcendentals=0),
    )(
        pending[:, 0], routes[:, 0, :, 0], probs[:, 0], saved_gate[:, 0, 0], saved_up[:, 0, 0],
        w_gate[0], w_up[0], w_down[0], jnp.transpose(w_router[0]),
    )
    return result[:, None]


def solution(mesh):
    in_specs = (
        P(None, "section", "expert", None),
        P(None, "section", "expert", None),
        P(None, "section", "expert"),
        P(None, "section", "expert", None, None, None),
        P(None, "section", "expert", None, None, None),
        P("section", None, "expert"),
        P("section", None, "expert"),
        P("section", "expert", None),
        P("section", None, None),
    )
    out_specs = P(None, "section", "expert", None)
    return jax.shard_map(
        per_device, mesh=mesh, in_specs=in_specs, out_specs=out_specs, check_vma=False
    )
```

```python
import functools

import jax
import jax.numpy as jnp
from jax import lax
from jax.experimental import pallas as pl
from jax.experimental.pallas import tpu as pltpu
from jax.sharding import PartitionSpec as P

MESH = pl.DeviceIdType.MESH
F32 = jnp.float32
BF16 = jnp.bfloat16
CHUNKS = 4


def dot(a, b, contract):
    return lax.dot_general(a, b, (contract, ((), ())), preferred_element_type=F32)


def layer_kernel(
    sections, experts, group, chunks,
    pend, routes, probs, gate, up, w_gate, w_up, w_down, router, out,
    grad, wgu, wd, picked, rows, p_own, p_got, parts, halves, sums, home, done,
    load_sem, out_sem, shift_send, shift_recv, p_send, p_recv, there_send, there_recv,
    fwd_send, fwd_recv, red_send, red_recv, back_send, back_recv,
):
    members = experts * group
    tokens, width = grad.shape[1], grad.shape[2]
    cap = tokens // experts
    step = width // chunks
    cols = [pl.ds(c * step, step) for c in range(chunks)]
    sec, me = lax.axis_index("section"), lax.axis_index("expert")
    mine, side = me // group, me % group
    odd = sec % 2
    way = (odd, 1 - odd)
    source = (sec + 1 - 2 * odd, lax.rem(sec + sections - 1 + 2 * odd, sections))

    def at(expert, member):
        return (sec, expert * group + member)

    def remote(src, dst, send, recv, device):
        return pltpu.make_async_remote_copy(
            src_ref=src, dst_ref=dst, send_sem=send, recv_sem=recv,
            device_id=device, device_id_type=MESH)

    loads = [
        pltpu.make_async_copy(w_down, wd, load_sem.at[0]),
        pltpu.make_async_copy(w_gate, wgu.at[:, pl.ds(0, w_gate.shape[1])], load_sem.at[1]),
        pltpu.make_async_copy(
            w_up, wgu.at[:, pl.ds(w_gate.shape[1], w_up.shape[1])], load_sem.at[2]),
    ]
    for load in loads:
        load.start()

    barrier = pltpu.get_barrier_semaphore()
    for other in source:
        pl.semaphore_signal(barrier, inc=1, device_id=(other, me), device_id_type=MESH)
    for k in range(1, members):
        pl.semaphore_signal(
            barrier, inc=1, device_id=(sec, lax.rem(me + k, members)), device_id_type=MESH)
    pl.semaphore_wait(barrier, members + 1)

    sent = []

    def shift(f, c):
        return remote(pend.at[1 - way[f], :, cols[c]], grad.at[f, :, cols[c]],
                      shift_send.at[f, c], shift_recv.at[f, c], (source[f], me))

    for f in range(2):
        for c in range(chunks):
            copy = shift(f, c)
            copy.start()
            sent.append(copy)

    table = []
    both_routes, both_probs = routes[...], probs[...].astype(F32)
    before = (lax.broadcasted_iota(jnp.int32, (tokens, tokens), 0)
              < lax.broadcasted_iota(jnp.int32, (tokens, tokens), 1)).astype(F32)
    for f in range(2):
        swap = odd == 1
        first, second = (0, 1) if f == 0 else (1, 0)
        r = jnp.where(swap, both_routes[second:second + 1], both_routes[first:first + 1])
        p = jnp.where(swap, both_probs[second:second + 1], both_probs[first:first + 1])
        named = (lax.broadcasted_iota(jnp.int32, (8, tokens), 0) == r).astype(F32)
        count = dot(named, before, ((1,), (0,)))
        slot = jnp.sum(named * count, axis=0, keepdims=True)
        dest = r.astype(F32) * cap + slot
        select = lax.broadcasted_iota(jnp.int32, (tokens, tokens), 0).astype(F32) == dest
        table.append(select.astype(F32).astype(BF16))
        p_slot = jnp.sum(jnp.where(select, p, 0.0), axis=1, keepdims=True)
        p_own[:, f] = jnp.broadcast_to(p_slot, (tokens, 128)).astype(BF16).reshape(
            experts, cap, 128)

    def p_copy(k):
        to = lax.rem(me + k, members)
        return remote(p_own.at[to // group], p_got.at[me], p_send.at[k], p_recv.at[k], (sec, to))

    p_got[me] = p_own[mine]
    for k in range(1, members):
        copy = p_copy(k)
        copy.start()
        sent.append(copy)

    def there(f, c, k):
        to = lax.rem(mine + k, experts)
        return remote(picked.at[f, to, :, cols[c]], rows.at[f, mine, side, :, cols[c]],
                      there_send.at[f, c, k], there_recv.at[f, c, k], at(to, side))

    def forward(f, c, k, m):
        band = lax.rem(mine + experts - k, experts)
        src = picked.at[f, mine, :, cols[c]] if k == 0 else rows.at[f, band, side, :, cols[c]]
        return remote(src, rows.at[f, band, side, :, cols[c]],
                      fwd_send.at[f, c, k, m], fwd_recv.at[f, c, k, m],
                      at(mine, lax.rem(side + m, group)))

    def reduce(f, c, m):
        to = lax.rem(side + m, group)
        return remote(parts.at[f, :, to, :, cols[c]], halves.at[f, m - 1, :, :, cols[c]],
                      red_send.at[f, c, m], red_recv.at[f, c, m], at(mine, to))

    def back(f, c, k):
        to = lax.rem(mine + k, experts)
        return remote(sums.at[f, to, :, cols[c]], home.at[f, mine, :, cols[c]],
                      back_send.at[f, c, k], back_recv.at[f, c, k], at(to, side))

    def start(copy):
        copy.start()
        sent.append(copy)

    def pick(f, c):
        shift(f, c).wait_recv()
        got = dot(table[f], grad[f, :, cols[c]], ((1,), (0,))).astype(BF16)
        picked[f, :, :, cols[c]] = got.reshape(experts, cap, step)
        for k in range(experts - 1, 0, -1):
            start(there(f, c, k))
        for m in range(1, group):
            start(forward(f, c, 0, m))
        rows[f, mine, side, :, cols[c]] = picked[f, mine, :, cols[c]]

    def pass_on(f, c):
        for k in range(1, experts):
            there(f, c, k).wait_recv()
            for m in range(1, group):
                start(forward(f, c, k, m))

    def inner(f, c, z):
        for k in range(experts):
            for m in range(1, group):
                forward(f, c, k, m).wait_recv()
        held = rows[f, :, :, :, cols[c]].reshape(members * cap, step)
        return z + dot(held, wd[:, cols[c]], ((1,), (1,)))

    def middle(f, z):
        a = gate[way[f]].reshape(members * cap, -1).astype(F32)
        b = up[way[f]].reshape(members * cap, -1).astype(F32)
        p = p_got[:, f].reshape(members * cap, 128)[:, 0:1].astype(F32)
        sg = jax.nn.sigmoid(a)
        product = jnp.sum(a * sg * b * z, axis=1, keepdims=True).astype(BF16).astype(F32)
        u = p * z
        grad_gate = (u * b * sg * (1.0 + a * (1.0 - sg))).astype(BF16)
        grad_up = (u * a * sg).astype(BF16)
        hidden = jnp.concatenate([grad_gate, grad_up], axis=1)
        return hidden, product * p * (1.0 - p)

    def outer(f, c, hidden, scaled):
        column = router[pl.ds(mine, 1), cols[c]]
        part = dot(hidden, wgu[cols[c], :], ((1,), (1,))) + scaled * column
        parts[f, :, :, :, cols[c]] = part.astype(BF16).reshape(experts, group, cap, step)
        for m in range(1, group):
            start(reduce(f, c, m))

    def add_up(f, c):
        total = parts[f, :, side, :, cols[c]].astype(F32)
        for m in range(1, group):
            reduce(f, c, m).wait_recv()
            total = total + halves[f, m - 1, :, :, cols[c]].astype(F32)
        sums[f, :, :, cols[c]] = total.astype(BF16)
        for k in range(experts - 1, 0, -1):
            start(back(f, c, k))
        home[f, mine, :, cols[c]] = sums[f, mine, :, cols[c]]

    def finish(f, c):
        for k in range(1, experts):
            back(f, c, k).wait_recv()
        got = dot(table[f], home[f, :, :, cols[c]].reshape(tokens, step), ((0,), (0,)))
        done[f, :, cols[c]] = (grad[f, :, cols[c]].astype(F32) + got).astype(BF16)
        copy = pltpu.make_async_copy(
            done.at[f, :, cols[c]], out.at[way[f], :, cols[c]], out_sem.at[f, c])
        copy.start()
        written.append(copy)

    written = []
    for c in range(chunks):
        pick(0, c)
    zero = jnp.zeros((members * cap, wd.shape[0]), F32)
    loads[0].wait()
    z = zero
    for c in range(chunks):
        pass_on(0, c)
        pick(1, c)
        if c > 0:
            z = inner(0, c - 1, z)
    z = inner(0, chunks - 1, z)
    for k in range(1, members):
        p_copy(k).wait_recv()
    hidden = middle(0, z)
    for load in loads[1:]:
        load.wait()
    for c in range(chunks):
        outer(0, c, *hidden)
    z = zero
    for c in range(chunks):
        pass_on(1, c)
        add_up(0, c)
        if c > 0:
            z = inner(1, c - 1, z)
    z = inner(1, chunks - 1, z)
    hidden = middle(1, z)
    for c in range(chunks):
        outer(1, c, *hidden)
    for c in range(chunks):
        finish(0, c)
        add_up(1, c)
    for c in range(chunks):
        finish(1, c)
    for copy in sent:
        copy.wait_send()
    for copy in written:
        copy.wait()


def copy_kernel(src, dst, sem):
    copies = [
        pltpu.make_async_copy(src.at[i, pl.ds(r, 16)], dst.at[i, pl.ds(r, 16)], sem.at[i, r // 16])
        for i in range(src.shape[0])
        for r in range(0, src.shape[1], 16)
    ]
    for copy in copies:
        copy.start()
    for copy in copies:
        copy.wait()


def per_device(pending, routes, probs, saved_gate, saved_up, w_gate, w_up, w_down, w_router):
    sections, members = lax.axis_size("section"), lax.axis_size("expert")
    experts = w_router.shape[2]
    group = members // experts
    tokens, width = pending.shape[2], pending.shape[3]
    cap = tokens // experts
    hidden = w_gate.shape[2]
    chunks = CHUNKS
    dma, vmem = pltpu.SemaphoreType.DMA, pltpu.VMEM
    any_spec = pl.BlockSpec(memory_space=pl.ANY)
    vmem_spec = pl.BlockSpec(memory_space=pltpu.VMEM)
    result = pl.pallas_call(
        functools.partial(layer_kernel, sections, experts, group, chunks),
        out_shape=jax.ShapeDtypeStruct((2, tokens, width), BF16),
        in_specs=[any_spec] + [vmem_spec] * 4 + [any_spec] * 3 + [vmem_spec],
        out_specs=any_spec,
        scratch_shapes=[
            vmem((2, tokens, width), BF16),
            vmem((width, 2 * hidden), BF16),
            vmem((hidden, width), BF16),
            vmem((2, experts, cap, width), BF16),
            vmem((2, experts, group, cap, width), BF16),
            vmem((experts, 2, cap, 128), BF16),
            vmem((members, 2, cap, 128), BF16),
            vmem((2, experts, group, cap, width), BF16),
            vmem((2, max(group - 1, 1), experts, cap, width), BF16),
            vmem((2, experts, cap, width), BF16),
            vmem((2, experts, cap, width), BF16),
            vmem((2, tokens, width), BF16),
            dma((3,)),
            dma((2, chunks)),
            dma((2, chunks)), dma((2, chunks)),
            dma((members,)), dma((members,)),
            dma((2, chunks, experts)), dma((2, chunks, experts)),
            dma((2, chunks, experts, group)), dma((2, chunks, experts, group)),
            dma((2, chunks, group)), dma((2, chunks, group)),
            dma((2, chunks, experts)), dma((2, chunks, experts)),
        ],
        compiler_params=pltpu.CompilerParams(
            collective_id=0, has_side_effects=True, vmem_limit_bytes=56 << 20),
        cost_estimate=pl.CostEstimate(
            flops=12 * members * cap * hidden * width, bytes_accessed=8 << 20, transcendentals=0),
    )(
        pending[:, 0], routes[:, 0, :, 0], probs[:, 0], saved_gate[:, 0, 0], saved_up[:, 0, 0],
        w_gate[0], w_up[0], w_down[0], jnp.transpose(w_router[0]),
    )
    result = pl.pallas_call(
        copy_kernel,
        out_shape=jax.ShapeDtypeStruct(result.shape, BF16),
        in_specs=[any_spec],
        out_specs=any_spec,
        scratch_shapes=[dma((2, tokens // 16))],
    )(result)
    return result[:, None]


def solution(mesh):
    in_specs = (
        P(None, "section", "expert", None),
        P(None, "section", "expert", None),
        P(None, "section", "expert"),
        P(None, "section", "expert", None, None, None),
        P(None, "section", "expert", None, None, None),
        P("section", None, "expert"),
        P("section", None, "expert"),
        P("section", "expert", None),
        P("section", None, None),
    )
    out_specs = P(None, "section", "expert", None)
    return jax.shard_map(
        per_device, mesh=mesh, in_specs=in_specs, out_specs=out_specs, check_vma=False
    )
```

```python
import functools

import jax
import jax.numpy as jnp
from jax import lax
from jax.experimental import pallas as pl
from jax.experimental.pallas import tpu as pltpu
from jax.sharding import PartitionSpec as P

MESH = pl.DeviceIdType.MESH
F32 = jnp.float32
BF16 = jnp.bfloat16
CHUNKS = 4


def dot(a, b, contract):
    return lax.dot_general(a, b, (contract, ((), ())), preferred_element_type=F32)


def layer_kernel(
    sections, experts, group, chunks,
    pend, routes, probs, gate, up, w_gate, w_up, w_down, router, out,
    grad, wgu, wd, picked, rows, p_own, p_got, parts, halves, sums, home, done, held,
    stage_sem, load_sem, out_sem, shift_send, shift_recv, p_send, p_recv, there_send, there_recv,
    fwd_send, fwd_recv, red_send, red_recv, back_send, back_recv,
):
    members = experts * group
    tokens, width = grad.shape[1], grad.shape[2]
    cap = tokens // experts
    step = width // chunks
    cols = [pl.ds(c * step, step) for c in range(chunks)]
    sec, me = lax.axis_index("section"), lax.axis_index("expert")
    mine, side = me // group, me % group
    odd = sec % 2
    way = (odd, 1 - odd)
    source = (sec + 1 - 2 * odd, lax.rem(sec + sections - 1 + 2 * odd, sections))

    def at(expert, member):
        return (sec, expert * group + member)

    def remote(src, dst, send, recv, device):
        return pltpu.make_async_remote_copy(
            src_ref=src, dst_ref=dst, send_sem=send, recv_sem=recv,
            device_id=device, device_id_type=MESH)

    stage = [
        pltpu.make_async_copy(pend.at[1 - way[f]], held.at[f], stage_sem.at[f]) for f in range(2)
    ]
    loads = [
        pltpu.make_async_copy(w_down, wd, load_sem.at[0]),
        pltpu.make_async_copy(w_gate, wgu.at[:, pl.ds(0, w_gate.shape[1])], load_sem.at[1]),
        pltpu.make_async_copy(
            w_up, wgu.at[:, pl.ds(w_gate.shape[1], w_up.shape[1])], load_sem.at[2]),
    ]
    for load in stage + loads:
        load.start()

    barrier = pltpu.get_barrier_semaphore()
    for other in source:
        pl.semaphore_signal(barrier, inc=1, device_id=(other, me), device_id_type=MESH)
    for k in range(1, members):
        pl.semaphore_signal(
            barrier, inc=1, device_id=(sec, lax.rem(me + k, members)), device_id_type=MESH)
    pl.semaphore_wait(barrier, members + 1)

    sent = []

    def shift(f, c):
        return remote(held.at[f, :, cols[c]], grad.at[f, :, cols[c]],
                      shift_send.at[f, c], shift_recv.at[f, c], (source[f], me))

    for f in range(2):
        stage[f].wait()
        for c in range(chunks):
            copy = shift(f, c)
            copy.start()
            sent.append(copy)

    table = []
    both_routes, both_probs = routes[...], probs[...].astype(F32)
    before = (lax.broadcasted_iota(jnp.int32, (tokens, tokens), 0)
              < lax.broadcasted_iota(jnp.int32, (tokens, tokens), 1)).astype(F32)
    for f in range(2):
        swap = odd == 1
        first, second = (0, 1) if f == 0 else (1, 0)
        r = jnp.where(swap, both_routes[second:second + 1], both_routes[first:first + 1])
        p = jnp.where(swap, both_probs[second:second + 1], both_probs[first:first + 1])
        named = (lax.broadcasted_iota(jnp.int32, (8, tokens), 0) == r).astype(F32)
        count = dot(named, before, ((1,), (0,)))
        slot = jnp.sum(named * count, axis=0, keepdims=True)
        dest = r.astype(F32) * cap + slot
        select = lax.broadcasted_iota(jnp.int32, (tokens, tokens), 0).astype(F32) == dest
        table.append(select.astype(F32).astype(BF16))
        p_slot = jnp.sum(jnp.where(select, p, 0.0), axis=1, keepdims=True)
        p_own[:, f] = jnp.broadcast_to(p_slot, (tokens, 128)).astype(BF16).reshape(
            experts, cap, 128)

    def p_copy(k):
        to = lax.rem(me + k, members)
        return remote(p_own.at[to // group], p_got.at[me], p_send.at[k], p_recv.at[k], (sec, to))

    p_got[me] = p_own[mine]
    for k in range(1, members):
        copy = p_copy(k)
        copy.start()
        sent.append(copy)

    def there(f, c, k):
        to = lax.rem(mine + k, experts)
        return remote(picked.at[f, to, :, cols[c]], rows.at[f, mine, side, :, cols[c]],
                      there_send.at[f, c, k], there_recv.at[f, c, k], at(to, side))

    def forward(f, c, k, m):
        band = lax.rem(mine + experts - k, experts)
        src = picked.at[f, mine, :, cols[c]] if k == 0 else rows.at[f, band, side, :, cols[c]]
        return remote(src, rows.at[f, band, side, :, cols[c]],
                      fwd_send.at[f, c, k, m], fwd_recv.at[f, c, k, m],
                      at(mine, lax.rem(side + m, group)))

    def reduce(f, c, m):
        to = lax.rem(side + m, group)
        return remote(parts.at[f, :, to, :, cols[c]], halves.at[f, m - 1, :, :, cols[c]],
                      red_send.at[f, c, m], red_recv.at[f, c, m], at(mine, to))

    def back(f, c, k):
        to = lax.rem(mine + k, experts)
        return remote(sums.at[f, to, :, cols[c]], home.at[f, mine, :, cols[c]],
                      back_send.at[f, c, k], back_recv.at[f, c, k], at(to, side))

    def start(copy):
        copy.start()
        sent.append(copy)

    def pick(f, c):
        shift(f, c).wait_recv()
        got = dot(table[f], grad[f, :, cols[c]], ((1,), (0,))).astype(BF16)
        picked[f, :, :, cols[c]] = got.reshape(experts, cap, step)
        for k in range(experts - 1, 0, -1):
            start(there(f, c, k))
        for m in range(1, group):
            start(forward(f, c, 0, m))
        rows[f, mine, side, :, cols[c]] = picked[f, mine, :, cols[c]]

    def pass_on(f, c):
        for k in range(1, experts):
            there(f, c, k).wait_recv()
            for m in range(1, group):
                start(forward(f, c, k, m))

    def inner(f, c, z):
        for k in range(experts):
            for m in range(1, group):
                forward(f, c, k, m).wait_recv()
        held = rows[f, :, :, :, cols[c]].reshape(members * cap, step)
        return z + dot(held, wd[:, cols[c]], ((1,), (1,)))

    def middle(f, z):
        a = gate[way[f]].reshape(members * cap, -1).astype(F32)
        b = up[way[f]].reshape(members * cap, -1).astype(F32)
        p = p_got[:, f].reshape(members * cap, 128)[:, 0:1].astype(F32)
        sg = jax.nn.sigmoid(a)
        product = jnp.sum(a * sg * b * z, axis=1, keepdims=True).astype(BF16).astype(F32)
        u = p * z
        grad_gate = (u * b * sg * (1.0 + a * (1.0 - sg))).astype(BF16)
        grad_up = (u * a * sg).astype(BF16)
        hidden = jnp.concatenate([grad_gate, grad_up], axis=1)
        return hidden, product * p * (1.0 - p)

    def outer(f, c, hidden, scaled):
        column = router[pl.ds(mine, 1), cols[c]]
        part = dot(hidden, wgu[cols[c], :], ((1,), (1,))) + scaled * column
        parts[f, :, :, :, cols[c]] = part.astype(BF16).reshape(experts, group, cap, step)
        for m in range(1, group):
            start(reduce(f, c, m))

    def add_up(f, c):
        total = parts[f, :, side, :, cols[c]].astype(F32)
        for m in range(1, group):
            reduce(f, c, m).wait_recv()
            total = total + halves[f, m - 1, :, :, cols[c]].astype(F32)
        sums[f, :, :, cols[c]] = total.astype(BF16)
        for k in range(experts - 1, 0, -1):
            start(back(f, c, k))
        home[f, mine, :, cols[c]] = sums[f, mine, :, cols[c]]

    def finish(f, c):
        for k in range(1, experts):
            back(f, c, k).wait_recv()
        got = dot(table[f], home[f, :, :, cols[c]].reshape(tokens, step), ((0,), (0,)))
        done[f, :, cols[c]] = (grad[f, :, cols[c]].astype(F32) + got).astype(BF16)
        copy = pltpu.make_async_copy(
            done.at[f, :, cols[c]], out.at[way[f], :, cols[c]], out_sem.at[f, c])
        copy.start()
        written.append(copy)

    written = []
    for c in range(chunks):
        pick(0, c)
    zero = jnp.zeros((members * cap, wd.shape[0]), F32)
    loads[0].wait()
    z = zero
    for c in range(chunks):
        pass_on(0, c)
        pick(1, c)
        if c > 0:
            z = inner(0, c - 1, z)
    z = inner(0, chunks - 1, z)
    for k in range(1, members):
        p_copy(k).wait_recv()
    hidden = middle(0, z)
    for load in loads[1:]:
        load.wait()
    for c in range(chunks):
        outer(0, c, *hidden)
    z = zero
    for c in range(chunks):
        pass_on(1, c)
        add_up(0, c)
        if c > 0:
            z = inner(1, c - 1, z)
    z = inner(1, chunks - 1, z)
    hidden = middle(1, z)
    for c in range(chunks):
        outer(1, c, *hidden)
    for c in range(chunks):
        finish(0, c)
        add_up(1, c)
    for c in range(chunks):
        finish(1, c)
    for copy in sent:
        copy.wait_send()
    for copy in written:
        copy.wait()


def copy_kernel(src, dst):
    dst[...] = src[...]


def per_device(pending, routes, probs, saved_gate, saved_up, w_gate, w_up, w_down, w_router):
    sections, members = lax.axis_size("section"), lax.axis_size("expert")
    experts = w_router.shape[2]
    group = members // experts
    tokens, width = pending.shape[2], pending.shape[3]
    cap = tokens // experts
    hidden = w_gate.shape[2]
    chunks = CHUNKS
    dma, vmem = pltpu.SemaphoreType.DMA, pltpu.VMEM
    any_spec = pl.BlockSpec(memory_space=pl.ANY)
    vmem_spec = pl.BlockSpec(memory_space=pltpu.VMEM)
    result = pl.pallas_call(
        functools.partial(layer_kernel, sections, experts, group, chunks),
        out_shape=jax.ShapeDtypeStruct((2, tokens, width), BF16),
        in_specs=[any_spec] + [vmem_spec] * 4 + [any_spec] * 3 + [vmem_spec],
        out_specs=any_spec,
        scratch_shapes=[
            vmem((2, tokens, width), BF16),
            vmem((width, 2 * hidden), BF16),
            vmem((hidden, width), BF16),
            vmem((2, experts, cap, width), BF16),
            vmem((2, experts, group, cap, width), BF16),
            vmem((experts, 2, cap, 128), BF16),
            vmem((members, 2, cap, 128), BF16),
            vmem((2, experts, group, cap, width), BF16),
            vmem((2, max(group - 1, 1), experts, cap, width), BF16),
            vmem((2, experts, cap, width), BF16),
            vmem((2, experts, cap, width), BF16),
            vmem((2, tokens, width), BF16),
            vmem((2, tokens, width), BF16),
            dma((2,)),
            dma((3,)),
            dma((2, chunks)),
            dma((2, chunks)), dma((2, chunks)),
            dma((members,)), dma((members,)),
            dma((2, chunks, experts)), dma((2, chunks, experts)),
            dma((2, chunks, experts, group)), dma((2, chunks, experts, group)),
            dma((2, chunks, group)), dma((2, chunks, group)),
            dma((2, chunks, experts)), dma((2, chunks, experts)),
        ],
        compiler_params=pltpu.CompilerParams(
            collective_id=0, has_side_effects=True, vmem_limit_bytes=56 << 20),
        cost_estimate=pl.CostEstimate(
            flops=12 * members * cap * hidden * width, bytes_accessed=8 << 20, transcendentals=0),
    )(
        pending[:, 0], routes[:, 0, :, 0], probs[:, 0], saved_gate[:, 0, 0], saved_up[:, 0, 0],
        w_gate[0], w_up[0], w_down[0], jnp.transpose(w_router[0]),
    )
    result = pl.pallas_call(
        copy_kernel,
        grid=(2, 2),
        out_shape=jax.ShapeDtypeStruct(result.shape, BF16),
        in_specs=[pl.BlockSpec((1, tokens // 2, width), lambda i, j: (i, j, 0))],
        out_specs=pl.BlockSpec((1, tokens // 2, width), lambda i, j: (i, j, 0)),
    )(result)
    return result[:, None]


def solution(mesh):
    in_specs = (
        P(None, "section", "expert", None),
        P(None, "section", "expert", None),
        P(None, "section", "expert"),
        P(None, "section", "expert", None, None, None),
        P(None, "section", "expert", None, None, None),
        P("section", None, "expert"),
        P("section", None, "expert"),
        P("section", "expert", None),
        P("section", None, None),
    )
    out_specs = P(None, "section", "expert", None)
    return jax.shard_map(
        per_device, mesh=mesh, in_specs=in_specs, out_specs=out_specs, check_vma=False
    )
```

```python
import functools

import jax
import jax.numpy as jnp
from jax import lax
from jax.experimental import pallas as pl
from jax.experimental.pallas import tpu as pltpu
from jax.sharding import PartitionSpec as P

MESH = pl.DeviceIdType.MESH
F32 = jnp.float32
BF16 = jnp.bfloat16
CHUNKS = 4
SHARED = 2


def dot(a, b, contract):
    return lax.dot_general(a, b, (contract, ((), ())), preferred_element_type=F32)


def layer_kernel(
    sections, experts, group, chunks, shared,
    pend, routes, probs, gate, up, w_gate, w_up, w_down, router, out,
    grad, wgu, wd, wall, z_out, z_got, picked, rows, p_own, p_got, parts, halves, sums, home, done, held,
    stage_sem, load_sem, out_sem, shift_send, shift_recv, p_send, p_recv, there_send, there_recv,
    fwd_send, fwd_recv, w_send, w_recv, z_send, z_recv, red_send, red_recv, back_send, back_recv,
):
    members = experts * group
    tokens, width = grad.shape[1], grad.shape[2]
    cap = tokens // experts
    step = width // chunks
    cols = [pl.ds(c * step, step) for c in range(chunks)]
    by_weights, by_rows = list(range(shared)), list(range(shared, chunks))
    order = by_rows + by_weights
    split = shared * step
    hidden = w_gate.shape[1]
    sec, me = lax.axis_index("section"), lax.axis_index("expert")
    mine, side = me // group, me % group
    odd = sec % 2
    way = (odd, 1 - odd)
    source = (sec + 1 - 2 * odd, lax.rem(sec + sections - 1 + 2 * odd, sections))

    def at(expert, member):
        return (sec, expert * group + member)

    def remote(src, dst, send, recv, device):
        return pltpu.make_async_remote_copy(
            src_ref=src, dst_ref=dst, send_sem=send, recv_sem=recv,
            device_id=device, device_id_type=MESH)

    stage = [
        pltpu.make_async_copy(pend.at[1 - way[f]], held.at[f], stage_sem.at[f]) for f in range(2)
    ]
    loads = [
        pltpu.make_async_copy(
            w_down.at[:, pl.ds(0, split)], wall.at[side], load_sem.at[3]),
        pltpu.make_async_copy(
            w_down.at[:, pl.ds(split, width - split)], wd, load_sem.at[0]),
        pltpu.make_async_copy(w_gate, wgu.at[:, pl.ds(0, w_gate.shape[1])], load_sem.at[1]),
        pltpu.make_async_copy(
            w_up, wgu.at[:, pl.ds(w_gate.shape[1], w_up.shape[1])], load_sem.at[2]),
    ]
    for load in stage + loads:
        load.start()

    barrier = pltpu.get_barrier_semaphore()
    for other in source:
        pl.semaphore_signal(barrier, inc=1, device_id=(other, me), device_id_type=MESH)
    for k in range(1, members):
        pl.semaphore_signal(
            barrier, inc=1, device_id=(sec, lax.rem(me + k, members)), device_id_type=MESH)
    pl.semaphore_wait(barrier, members + 1)

    sent = []

    def shift(f, c):
        return remote(held.at[f, :, cols[c]], grad.at[f, :, cols[c]],
                      shift_send.at[f, c], shift_recv.at[f, c], (source[f], me))

    def start(copy):
        copy.start()
        sent.append(copy)

    def share(c, m):
        return remote(wall.at[side, :, cols[c]], wall.at[side, :, cols[c]],
                      w_send.at[c, m], w_recv.at[c, m], at(mine, lax.rem(side + m, group)))

    for f in range(2):
        stage[f].wait()
        for c in order:
            start(shift(f, c))
        if f == 0:
            loads[0].wait()
            for c in by_weights:
                for m in range(1, group):
                    start(share(c, m))

    table = []
    both_routes, both_probs = routes[...], probs[...].astype(F32)
    before = (lax.broadcasted_iota(jnp.int32, (tokens, tokens), 0)
              < lax.broadcasted_iota(jnp.int32, (tokens, tokens), 1)).astype(F32)
    for f in range(2):
        swap = odd == 1
        first, second = (0, 1) if f == 0 else (1, 0)
        r = jnp.where(swap, both_routes[second:second + 1], both_routes[first:first + 1])
        p = jnp.where(swap, both_probs[second:second + 1], both_probs[first:first + 1])
        named = (lax.broadcasted_iota(jnp.int32, (8, tokens), 0) == r).astype(F32)
        count = dot(named, before, ((1,), (0,)))
        slot = jnp.sum(named * count, axis=0, keepdims=True)
        dest = r.astype(F32) * cap + slot
        select = lax.broadcasted_iota(jnp.int32, (tokens, tokens), 0).astype(F32) == dest
        table.append(select.astype(F32).astype(BF16))
        p_slot = jnp.sum(jnp.where(select, p, 0.0), axis=1, keepdims=True)
        p_own[:, f] = jnp.broadcast_to(p_slot, (tokens, 128)).astype(BF16).reshape(
            experts, cap, 128)

    def p_copy(k):
        to = lax.rem(me + k, members)
        return remote(p_own.at[to // group], p_got.at[me], p_send.at[k], p_recv.at[k], (sec, to))

    p_got[me] = p_own[mine]
    for k in range(1, members):
        copy = p_copy(k)
        copy.start()
        sent.append(copy)

    def there(f, c, k):
        to = lax.rem(mine + k, experts)
        return remote(picked.at[f, to, :, cols[c]], rows.at[f, mine, side, :, cols[c]],
                      there_send.at[f, c, k], there_recv.at[f, c, k], at(to, side))

    def forward(f, c, k, m):
        band = lax.rem(mine + experts - k, experts)
        src = picked.at[f, mine, :, cols[c]] if k == 0 else rows.at[f, band, side, :, cols[c]]
        return remote(src, rows.at[f, band, side, :, cols[c]],
                      fwd_send.at[f, c, k, m], fwd_recv.at[f, c, k, m],
                      at(mine, lax.rem(side + m, group)))

    def reduce(f, c, m):
        to = lax.rem(side + m, group)
        return remote(parts.at[f, :, to, :, cols[c]], halves.at[f, m - 1, :, :, cols[c]],
                      red_send.at[f, c, m], red_recv.at[f, c, m], at(mine, to))

    def back(f, c, k):
        to = lax.rem(mine + k, experts)
        return remote(sums.at[f, to, :, cols[c]], home.at[f, mine, :, cols[c]],
                      back_send.at[f, c, k], back_recv.at[f, c, k], at(to, side))

    def swap_z(f, m):
        to = lax.rem(side + m, group)
        return remote(z_out.at[f, to], z_got.at[f, side],
                      z_send.at[f, m], z_recv.at[f, m], at(mine, to))

    def pick(f, c):
        shift(f, c).wait_recv()
        got = dot(table[f], grad[f, :, cols[c]], ((1,), (0,))).astype(BF16)
        picked[f, :, :, cols[c]] = got.reshape(experts, cap, step)
        for k in range(experts - 1, 0, -1):
            start(there(f, c, k))
        if c in by_rows:
            for m in range(1, group):
                start(forward(f, c, 0, m))
        rows[f, mine, side, :, cols[c]] = picked[f, mine, :, cols[c]]

    def pass_on(f, c):
        for k in range(1, experts):
            there(f, c, k).wait_recv()
            for m in range(1, group):
                start(forward(f, c, k, m))

    def beside(f):
        total = jnp.zeros((tokens, group * hidden), F32)
        for c in by_weights:
            if f == 0:
                for m in range(1, group):
                    share(c, m).wait_recv()
            for k in range(1, experts):
                there(f, c, k).wait_recv()
            own = rows[f, :, side, :, cols[c]].reshape(tokens, step)
            weights = wall[:, :, cols[c]].reshape(group * hidden, step)
            total = total + dot(own, weights, ((1,), (1,)))
        for j in range(group):
            z_out[f, j] = total[:, j * hidden:(j + 1) * hidden]
        for m in range(1, group):
            start(swap_z(f, m))
        z_got[f, side] = z_out[f, side]

    def inner(f, c):
        for k in range(experts):
            for m in range(1, group):
                forward(f, c, k, m).wait_recv()
        held_rows = rows[f, :, :, :, cols[c]].reshape(members * cap, step)
        weights = wd[:, pl.ds(c * step - split, step)]
        return dot(held_rows, weights, ((1,), (1,)))

    def all_z(f, z):
        for m in range(1, group):
            swap_z(f, m).wait_recv()
        got = [z_got[f, j].reshape(experts, cap, hidden) for j in range(group)]
        return z + jnp.stack(got, axis=1).reshape(members * cap, hidden)

    def middle(f, z):
        a = gate[way[f]].reshape(members * cap, -1).astype(F32)
        b = up[way[f]].reshape(members * cap, -1).astype(F32)
        p = p_got[:, f].reshape(members * cap, 128)[:, 0:1].astype(F32)
        sg = jax.nn.sigmoid(a)
        product = jnp.sum(a * sg * b * z, axis=1, keepdims=True).astype(BF16).astype(F32)
        u = p * z
        grad_gate = (u * b * sg * (1.0 + a * (1.0 - sg))).astype(BF16)
        grad_up = (u * a * sg).astype(BF16)
        grads = jnp.concatenate([grad_gate, grad_up], axis=1)
        return grads, product * p * (1.0 - p)

    def outer(f, c, grads, scaled):
        column = router[pl.ds(mine, 1), cols[c]]
        part = dot(grads, wgu[cols[c], :], ((1,), (1,))) + scaled * column
        parts[f, :, :, :, cols[c]] = part.astype(BF16).reshape(experts, group, cap, step)
        for m in range(1, group):
            start(reduce(f, c, m))

    def add_up(f, c):
        total = parts[f, :, side, :, cols[c]].astype(F32)
        for m in range(1, group):
            reduce(f, c, m).wait_recv()
            total = total + halves[f, m - 1, :, :, cols[c]].astype(F32)
        sums[f, :, :, cols[c]] = total.astype(BF16)
        for k in range(experts - 1, 0, -1):
            start(back(f, c, k))
        home[f, mine, :, cols[c]] = sums[f, mine, :, cols[c]]

    def finish(f, c):
        for k in range(1, experts):
            back(f, c, k).wait_recv()
        got = dot(table[f], home[f, :, :, cols[c]].reshape(tokens, step), ((0,), (0,)))
        done[f, :, cols[c]] = (grad[f, :, cols[c]].astype(F32) + got).astype(BF16)
        copy = pltpu.make_async_copy(
            done.at[f, :, cols[c]], out.at[way[f], :, cols[c]], out_sem.at[f, c])
        copy.start()
        written.append(copy)

    written = []
    for c in order:
        pick(0, c)
    for i, c in enumerate(order):
        if c in by_rows:
            pass_on(0, c)
        pick(1, c)
    for load in loads[1:]:
        load.wait()
    beside(0)
    pass_on(1, by_rows[0])
    z = jnp.zeros((members * cap, hidden), F32)
    for c in by_rows:
        z = z + inner(0, c)
    for k in range(1, members):
        p_copy(k).wait_recv()
    grads = middle(0, all_z(0, z))
    for c in range(chunks):
        outer(0, c, *grads)
    for c in by_rows[1:]:
        pass_on(1, c)
    beside(1)
    add_up(0, 0)
    z = jnp.zeros((members * cap, hidden), F32)
    for c in by_rows:
        z = z + inner(1, c)
    grads = middle(1, all_z(1, z))
    for c in range(chunks):
        outer(1, c, *grads)
    for c in range(1, chunks):
        add_up(0, c)
    for c in range(chunks):
        finish(0, c)
        add_up(1, c)
    for c in range(chunks):
        finish(1, c)
    for copy in sent:
        copy.wait_send()
    for copy in written:
        copy.wait()


def per_device(pending, routes, probs, saved_gate, saved_up, w_gate, w_up, w_down, w_router):
    sections, members = lax.axis_size("section"), lax.axis_size("expert")
    experts = w_router.shape[2]
    group = members // experts
    tokens, width = pending.shape[2], pending.shape[3]
    cap = tokens // experts
    hidden = w_gate.shape[2]
    chunks = CHUNKS
    split = SHARED * (width // chunks)
    dma, vmem = pltpu.SemaphoreType.DMA, pltpu.VMEM
    any_spec = pl.BlockSpec(memory_space=pl.ANY)
    vmem_spec = pl.BlockSpec(memory_space=pltpu.VMEM)
    result = pl.pallas_call(
        functools.partial(layer_kernel, sections, experts, group, chunks, SHARED),
        out_shape=jax.ShapeDtypeStruct((2, tokens, width), BF16),
        in_specs=[any_spec] + [vmem_spec] * 4 + [any_spec] * 3 + [vmem_spec],
        out_specs=any_spec,
        scratch_shapes=[
            vmem((2, tokens, width), BF16),
            vmem((width, 2 * hidden), BF16),
            vmem((hidden, width - split), BF16),
            vmem((group, hidden, split), BF16),
            vmem((2, group, tokens, hidden), F32),
            vmem((2, group, tokens, hidden), F32),
            vmem((2, experts, cap, width), BF16),
            vmem((2, experts, group, cap, width), BF16),
            vmem((experts, 2, cap, 128), BF16),
            vmem((members, 2, cap, 128), BF16),
            vmem((2, experts, group, cap, width), BF16),
            vmem((2, max(group - 1, 1), experts, cap, width), BF16),
            vmem((2, experts, cap, width), BF16),
            vmem((2, experts, cap, width), BF16),
            vmem((2, tokens, width), BF16),
            vmem((2, tokens, width), BF16),
            dma((2,)),
            dma((4,)),
            dma((2, chunks)),
            dma((2, chunks)), dma((2, chunks)),
            dma((members,)), dma((members,)),
            dma((2, chunks, experts)), dma((2, chunks, experts)),
            dma((2, chunks, experts, group)), dma((2, chunks, experts, group)),
            dma((chunks, group)), dma((chunks, group)),
            dma((2, group)), dma((2, group)),
            dma((2, chunks, group)), dma((2, chunks, group)),
            dma((2, chunks, experts)), dma((2, chunks, experts)),
        ],
        compiler_params=pltpu.CompilerParams(
            collective_id=0, has_side_effects=True, vmem_limit_bytes=56 << 20),
        cost_estimate=pl.CostEstimate(
            flops=12 * members * cap * hidden * width, bytes_accessed=8 << 20, transcendentals=0),
    )(
        pending[:, 0], routes[:, 0, :, 0], probs[:, 0], saved_gate[:, 0, 0], saved_up[:, 0, 0],
        w_gate[0], w_up[0], w_down[0], jnp.transpose(w_router[0]),
    )
    return result[:, None]


def solution(mesh):
    in_specs = (
        P(None, "section", "expert", None),
        P(None, "section", "expert", None),
        P(None, "section", "expert"),
        P(None, "section", "expert", None, None, None),
        P(None, "section", "expert", None, None, None),
        P("section", None, "expert"),
        P("section", None, "expert"),
        P("section", "expert", None),
        P("section", None, None),
    )
    out_specs = P(None, "section", "expert", None)
    return jax.shard_map(
        per_device, mesh=mesh, in_specs=in_specs, out_specs=out_specs, check_vma=False
    )
```

```python
import functools

import jax
import jax.numpy as jnp
from jax import lax
from jax.experimental import pallas as pl
from jax.experimental.pallas import tpu as pltpu
from jax.sharding import PartitionSpec as P

MESH = pl.DeviceIdType.MESH
F32 = jnp.float32
BF16 = jnp.bfloat16
CHUNKS = 4
SHARED = 2


def dot(a, b, contract):
    return lax.dot_general(a, b, (contract, ((), ())), preferred_element_type=F32)


def layer_kernel(
    sections, experts, group, chunks, shared,
    pend, routes, probs, gate, up, w_gate, w_up, w_down, router, out,
    grad, wgu, wd, wall, z_out, z_got, picked, rows, p_own, p_got, parts, halves, sums, home, done, held,
    stage_sem, load_sem, out_sem, shift_send, shift_recv, p_send, p_recv, there_send, there_recv,
    fwd_send, fwd_recv, w_send, w_recv, z_send, z_recv, red_send, red_recv, back_send, back_recv,
):
    members = experts * group
    tokens, width = grad.shape[1], grad.shape[2]
    cap = tokens // experts
    step = width // chunks
    cols = [pl.ds(c * step, step) for c in range(chunks)]
    by_weights, by_rows = list(range(shared)), list(range(shared, chunks))
    order = by_rows + by_weights
    split = shared * step
    hidden = w_gate.shape[1]
    sec, me = lax.axis_index("section"), lax.axis_index("expert")
    mine, side = me // group, me % group
    odd = sec % 2
    way = (odd, 1 - odd)
    source = (sec + 1 - 2 * odd, lax.rem(sec + sections - 1 + 2 * odd, sections))

    def at(expert, member):
        return (sec, expert * group + member)

    def remote(src, dst, send, recv, device):
        return pltpu.make_async_remote_copy(
            src_ref=src, dst_ref=dst, send_sem=send, recv_sem=recv,
            device_id=device, device_id_type=MESH)

    stage = [
        pltpu.make_async_copy(pend.at[1 - way[f]], held.at[f], stage_sem.at[f]) for f in range(2)
    ]
    loads = [
        pltpu.make_async_copy(
            w_down.at[:, pl.ds(0, split)], wall.at[side], load_sem.at[3]),
        pltpu.make_async_copy(
            w_down.at[:, pl.ds(split, width - split)], wd, load_sem.at[0]),
        pltpu.make_async_copy(w_gate, wgu.at[:, pl.ds(0, w_gate.shape[1])], load_sem.at[1]),
        pltpu.make_async_copy(
            w_up, wgu.at[:, pl.ds(w_gate.shape[1], w_up.shape[1])], load_sem.at[2]),
    ]
    for load in stage + loads:
        load.start()

    barrier = pltpu.get_barrier_semaphore()
    for other in source:
        pl.semaphore_signal(barrier, inc=1, device_id=(other, me), device_id_type=MESH)
    for k in range(1, members):
        pl.semaphore_signal(
            barrier, inc=1, device_id=(sec, lax.rem(me + k, members)), device_id_type=MESH)
    pl.semaphore_wait(barrier, members + 1)

    sent = []

    def shift(f, c):
        return remote(held.at[f, :, cols[c]], grad.at[f, :, cols[c]],
                      shift_send.at[f, c], shift_recv.at[f, c], (source[f], me))

    def start(copy):
        copy.start()
        sent.append(copy)

    def share(c, m):
        return remote(wall.at[side, :, cols[c]], wall.at[side, :, cols[c]],
                      w_send.at[c, m], w_recv.at[c, m], at(mine, lax.rem(side + m, group)))

    for f in range(2):
        stage[f].wait()
        for c in order:
            start(shift(f, c))
        if f == 0:
            loads[0].wait()
            for c in by_weights:
                for m in range(1, group):
                    start(share(c, m))

    table = []
    both_routes, both_probs = routes[...], probs[...].astype(F32)
    before = (lax.broadcasted_iota(jnp.int32, (tokens, tokens), 0)
              < lax.broadcasted_iota(jnp.int32, (tokens, tokens), 1)).astype(F32)
    for f in range(2):
        swap = odd == 1
        first, second = (0, 1) if f == 0 else (1, 0)
        r = jnp.where(swap, both_routes[second:second + 1], both_routes[first:first + 1])
        p = jnp.where(swap, both_probs[second:second + 1], both_probs[first:first + 1])
        named = (lax.broadcasted_iota(jnp.int32, (8, tokens), 0) == r).astype(F32)
        count = dot(named, before, ((1,), (0,)))
        slot = jnp.sum(named * count, axis=0, keepdims=True)
        dest = r.astype(F32) * cap + slot
        select = lax.broadcasted_iota(jnp.int32, (tokens, tokens), 0).astype(F32) == dest
        table.append(select.astype(F32).astype(BF16))
        p_slot = jnp.sum(jnp.where(select, p, 0.0), axis=1, keepdims=True)
        p_own[:, f] = jnp.broadcast_to(p_slot, (tokens, 128)).astype(BF16).reshape(
            experts, cap, 128)

    def p_copy(k):
        to = lax.rem(me + k, members)
        return remote(p_own.at[to // group], p_got.at[me], p_send.at[k], p_recv.at[k], (sec, to))

    p_got[me] = p_own[mine]
    for k in range(1, members):
        copy = p_copy(k)
        copy.start()
        sent.append(copy)

    def there(f, c, k):
        to = lax.rem(mine + k, experts)
        return remote(picked.at[f, to, :, cols[c]], rows.at[f, mine, side, :, cols[c]],
                      there_send.at[f, c, k], there_recv.at[f, c, k], at(to, side))

    def forward(f, c, k, m):
        band = lax.rem(mine + experts - k, experts)
        src = picked.at[f, mine, :, cols[c]] if k == 0 else rows.at[f, band, side, :, cols[c]]
        return remote(src, rows.at[f, band, side, :, cols[c]],
                      fwd_send.at[f, c, k, m], fwd_recv.at[f, c, k, m],
                      at(mine, lax.rem(side + m, group)))

    def reduce(f, c, m):
        to = lax.rem(side + m, group)
        return remote(parts.at[f, :, to, :, cols[c]], halves.at[f, m - 1, :, :, cols[c]],
                      red_send.at[f, c, m], red_recv.at[f, c, m], at(mine, to))

    def back(f, c, k):
        to = lax.rem(mine + k, experts)
        return remote(sums.at[f, to, :, cols[c]], home.at[f, mine, :, cols[c]],
                      back_send.at[f, c, k], back_recv.at[f, c, k], at(to, side))

    def swap_z(f, m):
        to = lax.rem(side + m, group)
        return remote(z_out.at[f, to], z_got.at[f, side],
                      z_send.at[f, m], z_recv.at[f, m], at(mine, to))

    def pick(f, c):
        shift(f, c).wait_recv()
        got = dot(table[f], grad[f, :, cols[c]], ((1,), (0,))).astype(BF16)
        picked[f, :, :, cols[c]] = got.reshape(experts, cap, step)
        for k in range(experts - 1, 0, -1):
            start(there(f, c, k))
        if c in by_rows:
            for m in range(1, group):
                start(forward(f, c, 0, m))
        rows[f, mine, side, :, cols[c]] = picked[f, mine, :, cols[c]]

    def pass_on(f, c):
        for k in range(1, experts):
            there(f, c, k).wait_recv()
            for m in range(1, group):
                start(forward(f, c, k, m))

    def beside(f):
        total = jnp.zeros((tokens, group * hidden), F32)
        for c in by_weights:
            if f == 0:
                for m in range(1, group):
                    share(c, m).wait_recv()
            for k in range(1, experts):
                there(f, c, k).wait_recv()
            own = rows[f, :, side, :, cols[c]].reshape(tokens, step)
            weights = wall[:, :, cols[c]].reshape(group * hidden, step)
            total = total + dot(own, weights, ((1,), (1,)))
        for j in range(group):
            z_out[f, j] = total[:, j * hidden:(j + 1) * hidden]
        for m in range(1, group):
            start(swap_z(f, m))
        z_got[f, side] = z_out[f, side]

    def inner(f, c):
        for k in range(experts):
            for m in range(1, group):
                forward(f, c, k, m).wait_recv()
        held_rows = rows[f, :, :, :, cols[c]].reshape(members * cap, step)
        weights = wd[:, pl.ds(c * step - split, step)]
        return dot(held_rows, weights, ((1,), (1,)))

    def all_z(f, z):
        for m in range(1, group):
            swap_z(f, m).wait_recv()
        got = [z_got[f, j].reshape(experts, cap, hidden) for j in range(group)]
        return z + jnp.stack(got, axis=1).reshape(members * cap, hidden)

    def middle(f, z):
        a = gate[way[f]].reshape(members * cap, -1).astype(F32)
        b = up[way[f]].reshape(members * cap, -1).astype(F32)
        p = p_got[:, f].reshape(members * cap, 128)[:, 0:1].astype(F32)
        sg = jax.nn.sigmoid(a)
        product = jnp.sum(a * sg * b * z, axis=1, keepdims=True).astype(BF16).astype(F32)
        u = p * z
        grad_gate = (u * b * sg * (1.0 + a * (1.0 - sg))).astype(BF16)
        grad_up = (u * a * sg).astype(BF16)
        grads = jnp.concatenate([grad_gate, grad_up], axis=1)
        return grads, product * p * (1.0 - p)

    def outer(f, c, grads, scaled):
        column = router[pl.ds(mine, 1), cols[c]]
        part = dot(grads, wgu[cols[c], :], ((1,), (1,))) + scaled * column
        parts[f, :, :, :, cols[c]] = part.astype(BF16).reshape(experts, group, cap, step)
        for m in range(1, group):
            start(reduce(f, c, m))

    def add_up(f, c):
        total = parts[f, :, side, :, cols[c]].astype(F32)
        for m in range(1, group):
            reduce(f, c, m).wait_recv()
            total = total + halves[f, m - 1, :, :, cols[c]].astype(F32)
        sums[f, :, :, cols[c]] = total.astype(BF16)
        for k in range(experts - 1, 0, -1):
            start(back(f, c, k))
        home[f, mine, :, cols[c]] = sums[f, mine, :, cols[c]]

    def finish(f, c):
        for k in range(1, experts):
            back(f, c, k).wait_recv()
        got = dot(table[f], home[f, :, :, cols[c]].reshape(tokens, step), ((0,), (0,)))
        done[f, :, cols[c]] = (grad[f, :, cols[c]].astype(F32) + got).astype(BF16)
        copy = pltpu.make_async_copy(
            done.at[f, :, cols[c]], out.at[way[f], :, cols[c]], out_sem.at[f, c])
        copy.start()
        written.append(copy)

    written = []
    for c in order:
        pick(0, c)
    for i, c in enumerate(order):
        if c in by_rows:
            pass_on(0, c)
        pick(1, c)
    for load in loads[1:]:
        load.wait()
    beside(0)
    pass_on(1, by_rows[0])
    z = jnp.zeros((members * cap, hidden), F32)
    for c in by_rows:
        z = z + inner(0, c)
    for k in range(1, members):
        p_copy(k).wait_recv()
    grads = middle(0, all_z(0, z))
    for c in range(chunks):
        outer(0, c, *grads)
    for c in by_rows[1:]:
        pass_on(1, c)
    add_up(0, 0)
    beside(1)
    add_up(0, 1)
    z = jnp.zeros((members * cap, hidden), F32)
    for c in by_rows:
        z = z + inner(1, c)
    add_up(0, 2)
    grads = middle(1, all_z(1, z))
    for c in range(chunks):
        outer(1, c, *grads)
        if c == 1:
            for d in range(3, chunks):
                add_up(0, d)
    for c in range(chunks):
        finish(0, c)
        add_up(1, c)
    for c in range(chunks):
        finish(1, c)
    for copy in sent:
        copy.wait_send()
    for copy in written:
        copy.wait()


def per_device(pending, routes, probs, saved_gate, saved_up, w_gate, w_up, w_down, w_router):
    sections, members = lax.axis_size("section"), lax.axis_size("expert")
    experts = w_router.shape[2]
    group = members // experts
    tokens, width = pending.shape[2], pending.shape[3]
    cap = tokens // experts
    hidden = w_gate.shape[2]
    chunks = CHUNKS
    split = SHARED * (width // chunks)
    dma, vmem = pltpu.SemaphoreType.DMA, pltpu.VMEM
    any_spec = pl.BlockSpec(memory_space=pl.ANY)
    vmem_spec = pl.BlockSpec(memory_space=pltpu.VMEM)
    result = pl.pallas_call(
        functools.partial(layer_kernel, sections, experts, group, chunks, SHARED),
        out_shape=jax.ShapeDtypeStruct((2, tokens, width), BF16),
        in_specs=[any_spec] + [vmem_spec] * 4 + [any_spec] * 3 + [vmem_spec],
        out_specs=any_spec,
        scratch_shapes=[
            vmem((2, tokens, width), BF16),
            vmem((width, 2 * hidden), BF16),
            vmem((hidden, width - split), BF16),
            vmem((group, hidden, split), BF16),
            vmem((2, group, tokens, hidden), F32),
            vmem((2, group, tokens, hidden), F32),
            vmem((2, experts, cap, width), BF16),
            vmem((2, experts, group, cap, width), BF16),
            vmem((experts, 2, cap, 128), BF16),
            vmem((members, 2, cap, 128), BF16),
            vmem((2, experts, group, cap, width), BF16),
            vmem((2, max(group - 1, 1), experts, cap, width), BF16),
            vmem((2, experts, cap, width), BF16),
            vmem((2, experts, cap, width), BF16),
            vmem((2, tokens, width), BF16),
            vmem((2, tokens, width), BF16),
            dma((2,)),
            dma((4,)),
            dma((2, chunks)),
            dma((2, chunks)), dma((2, chunks)),
            dma((members,)), dma((members,)),
            dma((2, chunks, experts)), dma((2, chunks, experts)),
            dma((2, chunks, experts, group)), dma((2, chunks, experts, group)),
            dma((chunks, group)), dma((chunks, group)),
            dma((2, group)), dma((2, group)),
            dma((2, chunks, group)), dma((2, chunks, group)),
            dma((2, chunks, experts)), dma((2, chunks, experts)),
        ],
        compiler_params=pltpu.CompilerParams(
            collective_id=0, has_side_effects=True, vmem_limit_bytes=56 << 20),
        cost_estimate=pl.CostEstimate(
            flops=12 * members * cap * hidden * width, bytes_accessed=8 << 20, transcendentals=0),
    )(
        pending[:, 0], routes[:, 0, :, 0], probs[:, 0], saved_gate[:, 0, 0], saved_up[:, 0, 0],
        w_gate[0], w_up[0], w_down[0], jnp.transpose(w_router[0]),
    )
    return result[:, None]


def solution(mesh):
    in_specs = (
        P(None, "section", "expert", None),
        P(None, "section", "expert", None),
        P(None, "section", "expert"),
        P(None, "section", "expert", None, None, None),
        P(None, "section", "expert", None, None, None),
        P("section", None, "expert"),
        P("section", None, "expert"),
        P("section", "expert", None),
        P("section", None, None),
    )
    out_specs = P(None, "section", "expert", None)
    return jax.shard_map(
        per_device, mesh=mesh, in_specs=in_specs, out_specs=out_specs, check_vma=False
    )
```

```python
import functools

import jax
import jax.numpy as jnp
import numpy as np
from jax import lax
from jax.experimental import pallas as pl
from jax.experimental.pallas import tpu as pltpu
from jax.sharding import PartitionSpec as P

MESH = pl.DeviceIdType.MESH
F32 = jnp.float32
BF16 = jnp.bfloat16
IN_CUT = (7, 5, 8, 8)
OUT_CUT = ((7, 7, 7, 7), (8, 8, 6, 4, 2))
SHARED = 1


def dot(a, b, contract):
    return lax.dot_general(a, b, (contract, ((), ())), preferred_element_type=F32)


def layer_kernel(
    sections, experts, group,
    pend, routes, probs, gate, up, w_gate, w_up, w_down, router, out,
    grad, wgu, wd, wall, z_out, z_got, picked, rows, p_own, p_got, parts, halves, sums, home, done, held,
    stage_sem, load_sem, out_sem, shift_send, shift_recv, p_send, p_recv, there_send, there_recv,
    fwd_send, fwd_recv, w_send, w_recv, z_send, z_recv, red_send, red_recv, back_send, back_recv,
):
    members = experts * group
    tokens, width = grad.shape[1], grad.shape[2]
    cap = tokens // experts
    unit = width // sum(IN_CUT)

    def spans(cut):
        return [pl.ds(sum(cut[:c]) * unit, cut[c] * unit) for c in range(len(cut))]

    cols, ocols = spans(IN_CUT), [spans(cut) for cut in OUT_CUT]
    by_weights, by_rows = list(range(SHARED)), list(range(SHARED, len(cols)))
    order = by_rows + by_weights
    split = sum(IN_CUT[:SHARED]) * unit
    hidden = w_gate.shape[1]
    sec, me = lax.axis_index("section"), lax.axis_index("expert")
    mine, side = me // group, me % group
    odd = sec % 2
    way = (odd, 1 - odd)
    source = (sec + 1 - 2 * odd, lax.rem(sec + sections - 1 + 2 * odd, sections))

    def at(expert, member):
        return (sec, expert * group + member)

    def remote(src, dst, send, recv, device):
        return pltpu.make_async_remote_copy(
            src_ref=src, dst_ref=dst, send_sem=send, recv_sem=recv,
            device_id=device, device_id_type=MESH)

    stage = [
        pltpu.make_async_copy(pend.at[1 - way[f]], held.at[f], stage_sem.at[f]) for f in range(2)
    ]
    loads = [
        pltpu.make_async_copy(
            w_down.at[:, pl.ds(0, split)], wall.at[side], load_sem.at[3]),
        pltpu.make_async_copy(
            w_down.at[:, pl.ds(split, width - split)], wd, load_sem.at[0]),
        pltpu.make_async_copy(w_gate, wgu.at[:, pl.ds(0, w_gate.shape[1])], load_sem.at[1]),
        pltpu.make_async_copy(
            w_up, wgu.at[:, pl.ds(w_gate.shape[1], w_up.shape[1])], load_sem.at[2]),
    ]
    for load in stage + loads:
        load.start()

    barrier = pltpu.get_barrier_semaphore()
    for other in source:
        pl.semaphore_signal(barrier, inc=1, device_id=(other, me), device_id_type=MESH)
    for k in range(1, members):
        pl.semaphore_signal(
            barrier, inc=1, device_id=(sec, lax.rem(me + k, members)), device_id_type=MESH)
    pl.semaphore_wait(barrier, members + 1)

    sent = []

    def shift(f, c):
        return remote(held.at[f, :, cols[c]], grad.at[f, :, cols[c]],
                      shift_send.at[f, c], shift_recv.at[f, c], (source[f], me))

    def start(copy):
        copy.start()
        sent.append(copy)

    def share(c, m):
        return remote(wall.at[side, :, cols[c]], wall.at[side, :, cols[c]],
                      w_send.at[c, m], w_recv.at[c, m], at(mine, lax.rem(side + m, group)))

    for f in range(2):
        stage[f].wait()
        for c in order:
            start(shift(f, c))
        if f == 0:
            loads[0].wait()
            for c in by_weights:
                for m in range(1, group):
                    start(share(c, m))

    table = []
    both_routes, both_probs = routes[...], probs[...].astype(F32)
    before = (lax.broadcasted_iota(jnp.int32, (tokens, tokens), 0)
              < lax.broadcasted_iota(jnp.int32, (tokens, tokens), 1)).astype(F32)
    for f in range(2):
        swap = odd == 1
        first, second = (0, 1) if f == 0 else (1, 0)
        r = jnp.where(swap, both_routes[second:second + 1], both_routes[first:first + 1])
        p = jnp.where(swap, both_probs[second:second + 1], both_probs[first:first + 1])
        named = (lax.broadcasted_iota(jnp.int32, (8, tokens), 0) == r).astype(F32)
        count = dot(named, before, ((1,), (0,)))
        slot = jnp.sum(named * count, axis=0, keepdims=True)
        dest = r.astype(F32) * cap + slot
        select = lax.broadcasted_iota(jnp.int32, (tokens, tokens), 0).astype(F32) == dest
        table.append(select.astype(F32).astype(BF16))
        p_slot = jnp.sum(jnp.where(select, p, 0.0), axis=1, keepdims=True)
        p_own[:, f] = jnp.broadcast_to(p_slot, (tokens, 128)).astype(BF16).reshape(
            experts, cap, 128)

    def p_copy(k):
        to = lax.rem(me + k, members)
        return remote(p_own.at[to // group], p_got.at[me], p_send.at[k], p_recv.at[k], (sec, to))

    p_got[me] = p_own[mine]
    for k in range(1, members):
        copy = p_copy(k)
        copy.start()
        sent.append(copy)

    def there(f, c, k):
        to = lax.rem(mine + k, experts)
        return remote(picked.at[f, to, :, cols[c]], rows.at[f, mine, side, :, cols[c]],
                      there_send.at[f, c, k], there_recv.at[f, c, k], at(to, side))

    def forward(f, c, k, m):
        band = lax.rem(mine + experts - k, experts)
        src = picked.at[f, mine, :, cols[c]] if k == 0 else rows.at[f, band, side, :, cols[c]]
        return remote(src, rows.at[f, band, side, :, cols[c]],
                      fwd_send.at[f, c, k, m], fwd_recv.at[f, c, k, m],
                      at(mine, lax.rem(side + m, group)))

    def reduce(f, c, m):
        to = lax.rem(side + m, group)
        return remote(parts.at[f, :, to, :, ocols[f][c]], halves.at[f, m - 1, :, :, ocols[f][c]],
                      red_send.at[f, c, m], red_recv.at[f, c, m], at(mine, to))

    def back(f, c, k):
        to = lax.rem(mine + k, experts)
        return remote(sums.at[f, to, :, ocols[f][c]], home.at[f, mine, :, ocols[f][c]],
                      back_send.at[f, c, k], back_recv.at[f, c, k], at(to, side))

    def swap_z(f, m):
        to = lax.rem(side + m, group)
        return remote(z_out.at[f, to], z_got.at[f, side],
                      z_send.at[f, m], z_recv.at[f, m], at(mine, to))

    def pick(f, c):
        shift(f, c).wait_recv()
        got = dot(table[f], grad[f, :, cols[c]], ((1,), (0,))).astype(BF16)
        picked[f, :, :, cols[c]] = got.reshape(experts, cap, cols[c].size)
        for k in range(experts - 1, 0, -1):
            start(there(f, c, k))
        if c in by_rows:
            for m in range(1, group):
                start(forward(f, c, 0, m))
        rows[f, mine, side, :, cols[c]] = picked[f, mine, :, cols[c]]

    def pass_on(f, c):
        for k in range(1, experts):
            there(f, c, k).wait_recv()
            for m in range(1, group):
                start(forward(f, c, k, m))

    def beside(f):
        total = jnp.zeros((tokens, group * hidden), F32)
        for c in by_weights:
            if f == 0:
                for m in range(1, group):
                    share(c, m).wait_recv()
            for k in range(1, experts):
                there(f, c, k).wait_recv()
            own = rows[f, :, side, :, cols[c]].reshape(tokens, cols[c].size)
            weights = wall[:, :, cols[c]].reshape(group * hidden, cols[c].size)
            total = total + dot(own, weights, ((1,), (1,)))
        for j in range(group):
            z_out[f, j] = total[:, j * hidden:(j + 1) * hidden]
        for m in range(1, group):
            start(swap_z(f, m))
        z_got[f, side] = z_out[f, side]

    def inner(f, c):
        for k in range(experts):
            for m in range(1, group):
                forward(f, c, k, m).wait_recv()
        held_rows = rows[f, :, :, :, cols[c]].reshape(members * cap, cols[c].size)
        weights = wd[:, pl.ds(cols[c].start - split, cols[c].size)]
        return dot(held_rows, weights, ((1,), (1,)))

    def all_z(f, z):
        for m in range(1, group):
            swap_z(f, m).wait_recv()
        got = [z_got[f, j].reshape(experts, cap, hidden) for j in range(group)]
        return z + jnp.stack(got, axis=1).reshape(members * cap, hidden)

    def middle(f, z):
        a = gate[way[f]].reshape(members * cap, -1).astype(F32)
        b = up[way[f]].reshape(members * cap, -1).astype(F32)
        p = p_got[:, f].reshape(members * cap, 128)[:, 0:1].astype(F32)
        sg = jax.nn.sigmoid(a)
        product = jnp.sum(a * sg * b * z, axis=1, keepdims=True).astype(BF16).astype(F32)
        u = p * z
        grad_gate = (u * b * sg * (1.0 + a * (1.0 - sg))).astype(BF16)
        grad_up = (u * a * sg).astype(BF16)
        grads = jnp.concatenate([grad_gate, grad_up], axis=1)
        return grads, product * p * (1.0 - p)

    def outer(f, c, grads, scaled):
        column = router[pl.ds(mine, 1), ocols[f][c]]
        part = dot(grads, wgu[ocols[f][c], :], ((1,), (1,))) + scaled * column
        parts[f, :, :, :, ocols[f][c]] = part.astype(BF16).reshape(experts, group, cap, ocols[f][c].size)
        for m in range(1, group):
            start(reduce(f, c, m))

    def add_up(f, c):
        total = parts[f, :, side, :, ocols[f][c]].astype(F32)
        for m in range(1, group):
            reduce(f, c, m).wait_recv()
            total = total + halves[f, m - 1, :, :, ocols[f][c]].astype(F32)
        sums[f, :, :, ocols[f][c]] = total.astype(BF16)
        for k in range(experts - 1, 0, -1):
            start(back(f, c, k))
        home[f, mine, :, ocols[f][c]] = sums[f, mine, :, ocols[f][c]]

    def finish(f, c):
        for k in range(1, experts):
            back(f, c, k).wait_recv()
        got = dot(table[f], home[f, :, :, ocols[f][c]].reshape(tokens, ocols[f][c].size), ((0,), (0,)))
        done[f, :, ocols[f][c]] = (grad[f, :, ocols[f][c]].astype(F32) + got).astype(BF16)
        copy = pltpu.make_async_copy(
            done.at[f, :, ocols[f][c]], out.at[way[f], :, ocols[f][c]], out_sem.at[f, c])
        copy.start()
        written.append(copy)

    written = []
    last = [len(o) for o in ocols]
    for c in order:
        pick(0, c)
    for c in order:
        if c in by_rows:
            pass_on(0, c)
        pick(1, c)
    for load in loads[1:]:
        load.wait()
    beside(0)
    pass_on(1, by_rows[0])
    z = jnp.zeros((members * cap, hidden), F32)
    for c in by_rows:
        z = z + inner(0, c)
    for k in range(1, members):
        p_copy(k).wait_recv()
    grads = middle(0, all_z(0, z))
    for c in range(last[0]):
        outer(0, c, *grads)
    for c in by_rows[1:]:
        pass_on(1, c)
    add_up(0, 0)
    beside(1)
    add_up(0, 1)
    z = jnp.zeros((members * cap, hidden), F32)
    for c in by_rows:
        z = z + inner(1, c)
    add_up(0, 2)
    grads = middle(1, all_z(1, z))
    for c in range(last[1]):
        outer(1, c, *grads)
        if c == 1:
            for d in range(3, last[0]):
                add_up(0, d)
    for c in range(last[0]):
        finish(0, c)
        add_up(1, c)
    for c in range(last[0], last[1]):
        add_up(1, c)
    for c in range(last[1]):
        finish(1, c)
    for copy in sent:
        copy.wait_send()
    for copy in written:
        copy.wait()


def per_device(pending, routes, probs, saved_gate, saved_up, w_gate, w_up, w_down, w_router):
    sections, members = lax.axis_size("section"), lax.axis_size("expert")
    experts = w_router.shape[2]
    group = members // experts
    tokens, width = pending.shape[2], pending.shape[3]
    cap = tokens // experts
    hidden = w_gate.shape[2]
    chunks, pieces = len(IN_CUT), max(len(cut) for cut in OUT_CUT)
    split = sum(IN_CUT[:SHARED]) * (width // sum(IN_CUT))
    dma, vmem = pltpu.SemaphoreType.DMA, pltpu.VMEM
    any_spec = pl.BlockSpec(memory_space=pl.ANY)
    vmem_spec = pl.BlockSpec(memory_space=pltpu.VMEM)
    scratch = [
        vmem((2, tokens, width), BF16),
        vmem((width, 2 * hidden), BF16),
        vmem((hidden, width - split), BF16),
        vmem((group, hidden, split), BF16),
        vmem((2, group, tokens, hidden), F32),
        vmem((2, group, tokens, hidden), F32),
        vmem((2, experts, cap, width), BF16),
        vmem((2, experts, group, cap, width), BF16),
        vmem((experts, 2, cap, 128), BF16),
        vmem((members, 2, cap, 128), BF16),
        vmem((2, experts, group, cap, width), BF16),
        vmem((2, max(group - 1, 1), experts, cap, width), BF16),
        vmem((2, experts, cap, width), BF16),
        vmem((2, experts, cap, width), BF16),
        vmem((2, tokens, width), BF16),
        vmem((2, tokens, width), BF16),
        dma((2,)),
        dma((4,)),
        dma((2, pieces)),
        dma((2, chunks)), dma((2, chunks)),
        dma((members,)), dma((members,)),
        dma((2, chunks, experts)), dma((2, chunks, experts)),
        dma((2, chunks, experts, group)), dma((2, chunks, experts, group)),
        dma((chunks, group)), dma((chunks, group)),
        dma((2, group)), dma((2, group)),
        dma((2, pieces, group)), dma((2, pieces, group)),
        dma((2, pieces, experts)), dma((2, pieces, experts)),
    ]
    room = sum(
        int(np.prod(s.shape)) * s.dtype.itemsize for s in scratch if s.memory_space == pltpu.VMEM)
    result = pl.pallas_call(
        functools.partial(layer_kernel, sections, experts, group),
        out_shape=jax.ShapeDtypeStruct((2, tokens, width), BF16),
        in_specs=[any_spec] + [vmem_spec] * 4 + [any_spec] * 3 + [vmem_spec],
        out_specs=any_spec,
        scratch_shapes=scratch,
        compiler_params=pltpu.CompilerParams(
            collective_id=0, has_side_effects=True, vmem_limit_bytes=room + (8 << 20)),
        cost_estimate=pl.CostEstimate(
            flops=12 * members * cap * hidden * width, bytes_accessed=8 << 20, transcendentals=0),
    )(
        pending[:, 0], routes[:, 0, :, 0], probs[:, 0], saved_gate[:, 0, 0], saved_up[:, 0, 0],
        w_gate[0], w_up[0], w_down[0], jnp.transpose(w_router[0]),
    )
    return result[:, None]


def solution(mesh):
    in_specs = (
        P(None, "section", "expert", None),
        P(None, "section", "expert", None),
        P(None, "section", "expert"),
        P(None, "section", "expert", None, None, None),
        P(None, "section", "expert", None, None, None),
        P("section", None, "expert"),
        P("section", None, "expert"),
        P("section", "expert", None),
        P("section", None, None),
    )
    out_specs = P(None, "section", "expert", None)
    return jax.shard_map(
        per_device, mesh=mesh, in_specs=in_specs, out_specs=out_specs, check_vma=False
    )
```

```python
import functools

import jax
import jax.numpy as jnp
import numpy as np
from jax import lax
from jax.experimental import pallas as pl
from jax.experimental.pallas import tpu as pltpu
from jax.sharding import PartitionSpec as P

MESH = pl.DeviceIdType.MESH
F32 = jnp.float32
BF16 = jnp.bfloat16
IN_CUT = (7, 5, 8, 8)
OUT_CUT = ((7, 7, 7, 7), (8, 8, 6, 4, 2))
SHARED = 1


def dot(a, b, contract):
    return lax.dot_general(a, b, (contract, ((), ())), preferred_element_type=F32)


def layer_kernel(
    sections, experts, group,
    pend, routes_in, probs_in, gate_in, up_in, w_gate, w_up, w_down, router_in, out,
    routes, probs, gate, up, router,
    grad, wgu, wd, wall, z_out, z_got, picked, rows, p_own, p_got, parts, halves, sums, home, done, held,
    stage_sem, load_sem, small_sem, out_sem, shift_send, shift_recv, p_send, p_recv, there_send, there_recv,
    fwd_send, fwd_recv, w_send, w_recv, z_send, z_recv, red_send, red_recv, back_send, back_recv,
):
    members = experts * group
    tokens, width = grad.shape[1], grad.shape[2]
    cap = tokens // experts
    unit = width // sum(IN_CUT)

    def spans(cut):
        return [pl.ds(sum(cut[:c]) * unit, cut[c] * unit) for c in range(len(cut))]

    cols, ocols = spans(IN_CUT), [spans(cut) for cut in OUT_CUT]
    by_weights, by_rows = list(range(SHARED)), list(range(SHARED, len(cols)))
    order = by_rows + by_weights
    split = sum(IN_CUT[:SHARED]) * unit
    hidden = w_gate.shape[1]
    sec, me = lax.axis_index("section"), lax.axis_index("expert")
    mine, side = me // group, me % group
    odd = sec % 2
    way = (odd, 1 - odd)
    source = (sec + 1 - 2 * odd, lax.rem(sec + sections - 1 + 2 * odd, sections))

    def at(expert, member):
        return (sec, expert * group + member)

    def remote(src, dst, send, recv, device):
        return pltpu.make_async_remote_copy(
            src_ref=src, dst_ref=dst, send_sem=send, recv_sem=recv,
            device_id=device, device_id_type=MESH)

    stage = [
        pltpu.make_async_copy(pend.at[1 - way[f]], held.at[f], stage_sem.at[f]) for f in range(2)
    ]
    loads = [
        pltpu.make_async_copy(
            w_down.at[:, pl.ds(0, split)], wall.at[side], load_sem.at[3]),
        pltpu.make_async_copy(
            w_down.at[:, pl.ds(split, width - split)], wd, load_sem.at[0]),
        pltpu.make_async_copy(w_gate, wgu.at[:, pl.ds(0, w_gate.shape[1])], load_sem.at[1]),
        pltpu.make_async_copy(
            w_up, wgu.at[:, pl.ds(w_gate.shape[1], w_up.shape[1])], load_sem.at[2]),
    ]
    small = [
        pltpu.make_async_copy(src, dst, small_sem.at[i])
        for i, (src, dst) in enumerate((
            (routes_in, routes), (probs_in, probs), (gate_in, gate), (up_in, up),
            (router_in, router)))
    ]
    for load in stage + loads[:1] + small + loads[1:]:
        load.start()

    barrier = pltpu.get_barrier_semaphore()
    for other in source:
        pl.semaphore_signal(barrier, inc=1, device_id=(other, me), device_id_type=MESH)
    for k in range(1, members):
        pl.semaphore_signal(
            barrier, inc=1, device_id=(sec, lax.rem(me + k, members)), device_id_type=MESH)
    pl.semaphore_wait(barrier, members + 1)

    sent = []

    def shift(f, c):
        return remote(held.at[f, :, cols[c]], grad.at[f, :, cols[c]],
                      shift_send.at[f, c], shift_recv.at[f, c], (source[f], me))

    def start(copy):
        copy.start()
        sent.append(copy)

    def share(c, m):
        return remote(wall.at[side, :, cols[c]], wall.at[side, :, cols[c]],
                      w_send.at[c, m], w_recv.at[c, m], at(mine, lax.rem(side + m, group)))

    for f in range(2):
        stage[f].wait()
        for c in order:
            start(shift(f, c))
        if f == 0:
            loads[0].wait()
            for c in by_weights:
                for m in range(1, group):
                    start(share(c, m))

    table = []
    for load in small[:2]:
        load.wait()
    both_routes, both_probs = routes[...], probs[...].astype(F32)
    before = (lax.broadcasted_iota(jnp.int32, (tokens, tokens), 0)
              < lax.broadcasted_iota(jnp.int32, (tokens, tokens), 1)).astype(F32)
    for f in range(2):
        swap = odd == 1
        first, second = (0, 1) if f == 0 else (1, 0)
        r = jnp.where(swap, both_routes[second:second + 1], both_routes[first:first + 1])
        p = jnp.where(swap, both_probs[second:second + 1], both_probs[first:first + 1])
        named = (lax.broadcasted_iota(jnp.int32, (8, tokens), 0) == r).astype(F32)
        count = dot(named, before, ((1,), (0,)))
        slot = jnp.sum(named * count, axis=0, keepdims=True)
        dest = r.astype(F32) * cap + slot
        select = lax.broadcasted_iota(jnp.int32, (tokens, tokens), 0).astype(F32) == dest
        table.append(select.astype(F32).astype(BF16))
        p_slot = jnp.sum(jnp.where(select, p, 0.0), axis=1, keepdims=True)
        p_own[:, f] = jnp.broadcast_to(p_slot, (tokens, 128)).astype(BF16).reshape(
            experts, cap, 128)

    def p_copy(k):
        to = lax.rem(me + k, members)
        return remote(p_own.at[to // group], p_got.at[me], p_send.at[k], p_recv.at[k], (sec, to))

    p_got[me] = p_own[mine]
    for k in range(1, members):
        copy = p_copy(k)
        copy.start()
        sent.append(copy)

    def there(f, c, k):
        to = lax.rem(mine + k, experts)
        return remote(picked.at[f, to, :, cols[c]], rows.at[f, mine, side, :, cols[c]],
                      there_send.at[f, c, k], there_recv.at[f, c, k], at(to, side))

    def forward(f, c, k, m):
        band = lax.rem(mine + experts - k, experts)
        src = picked.at[f, mine, :, cols[c]] if k == 0 else rows.at[f, band, side, :, cols[c]]
        return remote(src, rows.at[f, band, side, :, cols[c]],
                      fwd_send.at[f, c, k, m], fwd_recv.at[f, c, k, m],
                      at(mine, lax.rem(side + m, group)))

    def reduce(f, c, m):
        to = lax.rem(side + m, group)
        return remote(parts.at[f, :, to, :, ocols[f][c]], halves.at[f, m - 1, :, :, ocols[f][c]],
                      red_send.at[f, c, m], red_recv.at[f, c, m], at(mine, to))

    def back(f, c, k):
        to = lax.rem(mine + k, experts)
        return remote(sums.at[f, to, :, ocols[f][c]], home.at[f, mine, :, ocols[f][c]],
                      back_send.at[f, c, k], back_recv.at[f, c, k], at(to, side))

    def swap_z(f, m):
        to = lax.rem(side + m, group)
        return remote(z_out.at[f, to], z_got.at[f, side],
                      z_send.at[f, m], z_recv.at[f, m], at(mine, to))

    def pick(f, c):
        shift(f, c).wait_recv()
        got = dot(table[f], grad[f, :, cols[c]], ((1,), (0,))).astype(BF16)
        picked[f, :, :, cols[c]] = got.reshape(experts, cap, cols[c].size)
        for k in range(experts - 1, 0, -1):
            start(there(f, c, k))
        if c in by_rows:
            for m in range(1, group):
                start(forward(f, c, 0, m))
        rows[f, mine, side, :, cols[c]] = picked[f, mine, :, cols[c]]

    def pass_on(f, c):
        for k in range(1, experts):
            there(f, c, k).wait_recv()
            for m in range(1, group):
                start(forward(f, c, k, m))

    def beside(f):
        total = jnp.zeros((tokens, group * hidden), F32)
        for c in by_weights:
            if f == 0:
                for m in range(1, group):
                    share(c, m).wait_recv()
            for k in range(1, experts):
                there(f, c, k).wait_recv()
            own = rows[f, :, side, :, cols[c]].reshape(tokens, cols[c].size)
            weights = wall[:, :, cols[c]].reshape(group * hidden, cols[c].size)
            total = total + dot(own, weights, ((1,), (1,)))
        for j in range(group):
            z_out[f, j] = total[:, j * hidden:(j + 1) * hidden]
        for m in range(1, group):
            start(swap_z(f, m))
        z_got[f, side] = z_out[f, side]

    def inner(f, c):
        for k in range(experts):
            for m in range(1, group):
                forward(f, c, k, m).wait_recv()
        held_rows = rows[f, :, :, :, cols[c]].reshape(members * cap, cols[c].size)
        weights = wd[:, pl.ds(cols[c].start - split, cols[c].size)]
        return dot(held_rows, weights, ((1,), (1,)))

    def all_z(f, z):
        for m in range(1, group):
            swap_z(f, m).wait_recv()
        got = [z_got[f, j].reshape(experts, cap, hidden) for j in range(group)]
        return z + jnp.stack(got, axis=1).reshape(members * cap, hidden)

    def middle(f, z):
        a = gate[way[f]].reshape(members * cap, -1).astype(F32)
        b = up[way[f]].reshape(members * cap, -1).astype(F32)
        p = p_got[:, f].reshape(members * cap, 128)[:, 0:1].astype(F32)
        sg = jax.nn.sigmoid(a)
        product = jnp.sum(a * sg * b * z, axis=1, keepdims=True).astype(BF16).astype(F32)
        u = p * z
        grad_gate = (u * b * sg * (1.0 + a * (1.0 - sg))).astype(BF16)
        grad_up = (u * a * sg).astype(BF16)
        grads = jnp.concatenate([grad_gate, grad_up], axis=1)
        return grads, product * p * (1.0 - p)

    def outer(f, c, grads, scaled):
        column = router[pl.ds(mine, 1), ocols[f][c]]
        part = dot(grads, wgu[ocols[f][c], :], ((1,), (1,))) + scaled * column
        parts[f, :, :, :, ocols[f][c]] = part.astype(BF16).reshape(experts, group, cap, ocols[f][c].size)
        for m in range(1, group):
            start(reduce(f, c, m))

    def add_up(f, c):
        total = parts[f, :, side, :, ocols[f][c]].astype(F32)
        for m in range(1, group):
            reduce(f, c, m).wait_recv()
            total = total + halves[f, m - 1, :, :, ocols[f][c]].astype(F32)
        sums[f, :, :, ocols[f][c]] = total.astype(BF16)
        for k in range(experts - 1, 0, -1):
            start(back(f, c, k))
        home[f, mine, :, ocols[f][c]] = sums[f, mine, :, ocols[f][c]]

    def finish(f, c):
        for k in range(1, experts):
            back(f, c, k).wait_recv()
        got = dot(table[f], home[f, :, :, ocols[f][c]].reshape(tokens, ocols[f][c].size), ((0,), (0,)))
        done[f, :, ocols[f][c]] = (grad[f, :, ocols[f][c]].astype(F32) + got).astype(BF16)
        copy = pltpu.make_async_copy(
            done.at[f, :, ocols[f][c]], out.at[way[f], :, ocols[f][c]], out_sem.at[f, c])
        copy.start()
        written.append(copy)

    written = []
    last = [len(o) for o in ocols]
    for c in order:
        pick(0, c)
    for c in order:
        if c in by_rows:
            pass_on(0, c)
        pick(1, c)
    for load in loads[1:] + small[2:]:
        load.wait()
    beside(0)
    pass_on(1, by_rows[0])
    z = jnp.zeros((members * cap, hidden), F32)
    for c in by_rows:
        z = z + inner(0, c)
    for k in range(1, members):
        p_copy(k).wait_recv()
    grads = middle(0, all_z(0, z))
    for c in range(last[0]):
        outer(0, c, *grads)
    for c in by_rows[1:]:
        pass_on(1, c)
    add_up(0, 0)
    beside(1)
    add_up(0, 1)
    z = jnp.zeros((members * cap, hidden), F32)
    for c in by_rows:
        z = z + inner(1, c)
    add_up(0, 2)
    grads = middle(1, all_z(1, z))
    for c in range(last[1]):
        outer(1, c, *grads)
        if c == 1:
            for d in range(3, last[0]):
                add_up(0, d)
    for c in range(last[0]):
        finish(0, c)
        add_up(1, c)
    for c in range(last[0], last[1]):
        add_up(1, c)
    for c in range(last[1]):
        finish(1, c)
    for copy in sent:
        copy.wait_send()
    for copy in written:
        copy.wait()


def per_device(pending, routes, probs, saved_gate, saved_up, w_gate, w_up, w_down, w_router):
    sections, members = lax.axis_size("section"), lax.axis_size("expert")
    experts = w_router.shape[2]
    group = members // experts
    tokens, width = pending.shape[2], pending.shape[3]
    cap = tokens // experts
    hidden = w_gate.shape[2]
    chunks, pieces = len(IN_CUT), max(len(cut) for cut in OUT_CUT)
    split = sum(IN_CUT[:SHARED]) * (width // sum(IN_CUT))
    dma, vmem = pltpu.SemaphoreType.DMA, pltpu.VMEM
    any_spec = pl.BlockSpec(memory_space=pl.ANY)
    scratch = [
        vmem((2, tokens), jnp.int32),
        vmem((2, tokens), BF16),
        vmem((2, members, cap, hidden), BF16),
        vmem((2, members, cap, hidden), BF16),
        vmem((experts, width), F32),
        vmem((2, tokens, width), BF16),
        vmem((width, 2 * hidden), BF16),
        vmem((hidden, width - split), BF16),
        vmem((group, hidden, split), BF16),
        vmem((2, group, tokens, hidden), F32),
        vmem((2, group, tokens, hidden), F32),
        vmem((2, experts, cap, width), BF16),
        vmem((2, experts, group, cap, width), BF16),
        vmem((experts, 2, cap, 128), BF16),
        vmem((members, 2, cap, 128), BF16),
        vmem((2, experts, group, cap, width), BF16),
        vmem((2, max(group - 1, 1), experts, cap, width), BF16),
        vmem((2, experts, cap, width), BF16),
        vmem((2, experts, cap, width), BF16),
        vmem((2, tokens, width), BF16),
        vmem((2, tokens, width), BF16),
        dma((2,)),
        dma((4,)),
        dma((5,)),
        dma((2, pieces)),
        dma((2, chunks)), dma((2, chunks)),
        dma((members,)), dma((members,)),
        dma((2, chunks, experts)), dma((2, chunks, experts)),
        dma((2, chunks, experts, group)), dma((2, chunks, experts, group)),
        dma((chunks, group)), dma((chunks, group)),
        dma((2, group)), dma((2, group)),
        dma((2, pieces, group)), dma((2, pieces, group)),
        dma((2, pieces, experts)), dma((2, pieces, experts)),
    ]
    room = sum(
        int(np.prod(s.shape)) * s.dtype.itemsize for s in scratch if s.memory_space == pltpu.VMEM)
    result = pl.pallas_call(
        functools.partial(layer_kernel, sections, experts, group),
        out_shape=jax.ShapeDtypeStruct((2, tokens, width), BF16),
        in_specs=[pl.BlockSpec(memory_space=pltpu.HBM)] * 9,
        out_specs=any_spec,
        scratch_shapes=scratch,
        compiler_params=pltpu.CompilerParams(
            collective_id=0, has_side_effects=True, vmem_limit_bytes=room + (8 << 20)),
        cost_estimate=pl.CostEstimate(
            flops=12 * members * cap * hidden * width, bytes_accessed=8 << 20, transcendentals=0),
    )(*[pltpu.with_memory_space_constraint(value, pltpu.HBM) for value in (
        pending[:, 0], routes[:, 0, :, 0], probs[:, 0], saved_gate[:, 0, 0], saved_up[:, 0, 0],
        w_gate[0], w_up[0], w_down[0], jnp.transpose(w_router[0]),
    )])
    return result[:, None]


def solution(mesh):
    in_specs = (
        P(None, "section", "expert", None),
        P(None, "section", "expert", None),
        P(None, "section", "expert"),
        P(None, "section", "expert", None, None, None),
        P(None, "section", "expert", None, None, None),
        P("section", None, "expert"),
        P("section", None, "expert"),
        P("section", "expert", None),
        P("section", None, None),
    )
    out_specs = P(None, "section", "expert", None)
    return jax.shard_map(
        per_device, mesh=mesh, in_specs=in_specs, out_specs=out_specs, check_vma=False
    )
```

```python
import functools

import jax
import jax.numpy as jnp
import numpy as np
from jax import lax
from jax.experimental import pallas as pl
from jax.experimental.pallas import tpu as pltpu
from jax.sharding import PartitionSpec as P

MESH = pl.DeviceIdType.MESH
F32 = jnp.float32
BF16 = jnp.bfloat16
IN_CUT = (7, 5, 8, 8)
OUT_CUT = ((7, 7, 7, 7), (8, 8, 6, 4, 2))
SHARED = 1


def dot(a, b, contract):
    return lax.dot_general(a, b, (contract, ((), ())), preferred_element_type=F32)


def layer_kernel(
    sections, experts, group,
    pend, routes_in, probs_in, gate_in, up_in, w_gate, w_up, w_down, router_in, out,
    routes, probs, gate, up, router,
    grad, wgu, wd, wall, z_out, z_got, picked, rows, p_own, p_got, parts, halves, sums, home, done, held,
    stage_sem, load_sem, small_sem, out_sem, shift_send, shift_recv, p_send, p_recv, there_send, there_recv,
    fwd_send, fwd_recv, w_send, w_recv, z_send, z_recv, red_send, red_recv, back_send, back_recv,
):
    members = experts * group
    tokens, width = grad.shape[1], grad.shape[2]
    cap = tokens // experts
    unit = width // sum(IN_CUT)

    def spans(cut):
        return [pl.ds(sum(cut[:c]) * unit, cut[c] * unit) for c in range(len(cut))]

    cols, ocols = spans(IN_CUT), [spans(cut) for cut in OUT_CUT]
    by_weights, by_rows = list(range(SHARED)), list(range(SHARED, len(cols)))
    order = by_rows + by_weights
    split = sum(IN_CUT[:SHARED]) * unit
    hidden = w_gate.shape[1]
    sec, me = lax.axis_index("section"), lax.axis_index("expert")
    mine, side = me // group, me % group
    odd = sec % 2
    way = (odd, 1 - odd)
    source = (sec + 1 - 2 * odd, lax.rem(sec + sections - 1 + 2 * odd, sections))

    def at(expert, member):
        return (sec, expert * group + member)

    def remote(src, dst, send, recv, device):
        return pltpu.make_async_remote_copy(
            src_ref=src, dst_ref=dst, send_sem=send, recv_sem=recv,
            device_id=device, device_id_type=MESH)

    stage = [
        pltpu.make_async_copy(pend.at[1 - way[f]], held.at[f], stage_sem.at[f]) for f in range(2)
    ]
    loads = [
        pltpu.make_async_copy(
            w_down.at[:, pl.ds(0, split)], wall.at[side], load_sem.at[3]),
        pltpu.make_async_copy(
            w_down.at[:, pl.ds(split, width - split)], wd, load_sem.at[0]),
        pltpu.make_async_copy(w_gate, wgu.at[:, pl.ds(0, w_gate.shape[1])], load_sem.at[1]),
        pltpu.make_async_copy(
            w_up, wgu.at[:, pl.ds(w_gate.shape[1], w_up.shape[1])], load_sem.at[2]),
    ]
    small = [
        pltpu.make_async_copy(src, dst, small_sem.at[i])
        for i, (src, dst) in enumerate((
            (routes_in, routes), (probs_in, probs), (gate_in, gate), (up_in, up),
            (router_in, router)))
    ]
    for load in stage + loads[:1] + small + loads[1:]:
        load.start()

    barrier = pltpu.get_barrier_semaphore()
    for other in source:
        pl.semaphore_signal(barrier, inc=1, device_id=(other, me), device_id_type=MESH)
    for k in range(1, members):
        pl.semaphore_signal(
            barrier, inc=1, device_id=(sec, lax.rem(me + k, members)), device_id_type=MESH)
    pl.semaphore_wait(barrier, members + 1)

    sent = []

    def shift(f, c):
        return remote(held.at[f, :, cols[c]], grad.at[f, :, cols[c]],
                      shift_send.at[f, c], shift_recv.at[f, c], (source[f], me))

    def start(copy):
        copy.start()
        sent.append(copy)

    def share(c, m):
        return remote(wall.at[side, :, cols[c]], wall.at[side, :, cols[c]],
                      w_send.at[c, m], w_recv.at[c, m], at(mine, lax.rem(side + m, group)))

    for f in range(2):
        stage[f].wait()
        for c in order:
            start(shift(f, c))
        if f == 0:
            loads[0].wait()
            for c in by_weights:
                for m in range(1, group):
                    start(share(c, m))

    table = []
    for load in small[:2]:
        load.wait()
    both_routes, both_probs = routes[...], probs[...].astype(F32)
    before = (lax.broadcasted_iota(jnp.int32, (tokens, tokens), 0)
              < lax.broadcasted_iota(jnp.int32, (tokens, tokens), 1)).astype(F32)
    for f in range(2):
        swap = odd == 1
        first, second = (0, 1) if f == 0 else (1, 0)
        r = jnp.where(swap, both_routes[second:second + 1], both_routes[first:first + 1])
        p = jnp.where(swap, both_probs[second:second + 1], both_probs[first:first + 1])
        named = (lax.broadcasted_iota(jnp.int32, (8, tokens), 0) == r).astype(F32)
        count = dot(named, before, ((1,), (0,)))
        slot = jnp.sum(named * count, axis=0, keepdims=True)
        dest = r.astype(F32) * cap + slot
        select = lax.broadcasted_iota(jnp.int32, (tokens, tokens), 0).astype(F32) == dest
        table.append(select.astype(F32).astype(BF16))
        p_slot = jnp.sum(jnp.where(select, p, 0.0), axis=1, keepdims=True)
        p_own[:, f] = jnp.broadcast_to(p_slot, (tokens, 128)).astype(BF16).reshape(
            experts, cap, 128)

    def p_copy(k):
        to = lax.rem(me + k, members)
        return remote(p_own.at[to // group], p_got.at[me], p_send.at[k], p_recv.at[k], (sec, to))

    p_got[me] = p_own[mine]
    for k in range(1, members):
        copy = p_copy(k)
        copy.start()
        sent.append(copy)

    def there(f, c, k):
        to = lax.rem(mine + k, experts)
        return remote(picked.at[f, to, :, cols[c]], rows.at[f, mine, side, :, cols[c]],
                      there_send.at[f, c, k], there_recv.at[f, c, k], at(to, side))

    def forward(f, c, k, m):
        band = lax.rem(mine + experts - k, experts)
        src = picked.at[f, mine, :, cols[c]] if k == 0 else rows.at[f, band, side, :, cols[c]]
        return remote(src, rows.at[f, band, side, :, cols[c]],
                      fwd_send.at[f, c, k, m], fwd_recv.at[f, c, k, m],
                      at(mine, lax.rem(side + m, group)))

    def reduce(f, c, m):
        to = lax.rem(side + m, group)
        return remote(parts.at[f, :, to, :, ocols[f][c]], halves.at[f, m - 1, :, :, ocols[f][c]],
                      red_send.at[f, c, m], red_recv.at[f, c, m], at(mine, to))

    def back(f, c, k):
        to = lax.rem(mine + k, experts)
        return remote(sums.at[f, to, :, ocols[f][c]], home.at[f, mine, :, ocols[f][c]],
                      back_send.at[f, c, k], back_recv.at[f, c, k], at(to, side))

    def swap_z(f, m):
        to = lax.rem(side + m, group)
        return remote(z_out.at[f, to], z_got.at[f, side],
                      z_send.at[f, m], z_recv.at[f, m], at(mine, to))

    def pick(f, c):
        shift(f, c).wait_recv()
        got = dot(table[f], grad[f, :, cols[c]], ((1,), (0,))).astype(BF16)
        picked[f, :, :, cols[c]] = got.reshape(experts, cap, cols[c].size)
        for k in range(experts - 1, 0, -1):
            start(there(f, c, k))
        if c in by_rows:
            for m in range(1, group):
                start(forward(f, c, 0, m))
        rows[f, mine, side, :, cols[c]] = picked[f, mine, :, cols[c]]

    def pass_on(f, c):
        for k in range(1, experts):
            there(f, c, k).wait_recv()
            for m in range(1, group):
                start(forward(f, c, k, m))

    def beside(f):
        total = jnp.zeros((tokens, group * hidden), F32)
        for c in by_weights:
            if f == 0:
                for m in range(1, group):
                    share(c, m).wait_recv()
            for k in range(1, experts):
                there(f, c, k).wait_recv()
            own = rows[f, :, side, :, cols[c]].reshape(tokens, cols[c].size)
            weights = wall[:, :, cols[c]].reshape(group * hidden, cols[c].size)
            total = total + dot(own, weights, ((1,), (1,)))
        for j in range(group):
            z_out[f, j] = total[:, j * hidden:(j + 1) * hidden]
        for m in range(1, group):
            start(swap_z(f, m))
        z_got[f, side] = z_out[f, side]

    def inner(f, c):
        for k in range(experts):
            for m in range(1, group):
                forward(f, c, k, m).wait_recv()
        held_rows = rows[f, :, :, :, cols[c]].reshape(members * cap, cols[c].size)
        weights = wd[:, pl.ds(cols[c].start - split, cols[c].size)]
        return dot(held_rows, weights, ((1,), (1,)))

    def all_z(f, z):
        for m in range(1, group):
            swap_z(f, m).wait_recv()
        got = [z_got[f, j].reshape(experts, cap, hidden) for j in range(group)]
        return z + jnp.stack(got, axis=1).reshape(members * cap, hidden)

    def middle(f, z):
        a = gate[way[f]].reshape(members * cap, -1).astype(F32)
        b = up[way[f]].reshape(members * cap, -1).astype(F32)
        p = p_got[:, f].reshape(members * cap, 128)[:, 0:1].astype(F32)
        sg = jax.nn.sigmoid(a)
        product = jnp.sum(a * sg * b * z, axis=1, keepdims=True).astype(BF16).astype(F32)
        u = p * z
        grad_gate = (u * b * sg * (1.0 + a * (1.0 - sg))).astype(BF16)
        grad_up = (u * a * sg).astype(BF16)
        grads = jnp.concatenate([grad_gate, grad_up], axis=1)
        return grads, product * p * (1.0 - p)

    def outer(f, c, grads, scaled):
        column = router[pl.ds(mine, 1), ocols[f][c]]
        part = dot(grads, wgu[ocols[f][c], :], ((1,), (1,))) + scaled * column
        parts[f, :, :, :, ocols[f][c]] = part.astype(BF16).reshape(experts, group, cap, ocols[f][c].size)
        for m in range(1, group):
            start(reduce(f, c, m))

    def add_up(f, c):
        total = parts[f, :, side, :, ocols[f][c]].astype(F32)
        for m in range(1, group):
            reduce(f, c, m).wait_recv()
            total = total + halves[f, m - 1, :, :, ocols[f][c]].astype(F32)
        sums[f, :, :, ocols[f][c]] = total.astype(BF16)
        for k in range(experts - 1, 0, -1):
            start(back(f, c, k))
        home[f, mine, :, ocols[f][c]] = sums[f, mine, :, ocols[f][c]]

    def finish(f, c):
        for k in range(1, experts):
            back(f, c, k).wait_recv()
        got = dot(table[f], home[f, :, :, ocols[f][c]].reshape(tokens, ocols[f][c].size), ((0,), (0,)))
        done[f, :, ocols[f][c]] = (grad[f, :, ocols[f][c]].astype(F32) + got).astype(BF16)
        copy = pltpu.make_async_copy(
            done.at[f, :, ocols[f][c]], out.at[way[f], :, ocols[f][c]], out_sem.at[f, c])
        copy.start()
        written.append(copy)

    written = []
    last = [len(o) for o in ocols]
    for c in order:
        pick(0, c)
    for c in order:
        if c in by_rows:
            pass_on(0, c)
        pick(1, c)
    for load in loads[1:] + small[2:]:
        load.wait()
    beside(0)
    pass_on(1, by_rows[0])
    z = jnp.zeros((members * cap, hidden), F32)
    for c in by_rows:
        z = z + inner(0, c)
    for k in range(1, members):
        p_copy(k).wait_recv()
    grads = middle(0, all_z(0, z))
    outer(0, 0, *grads)
    pass_on(1, by_rows[1])
    outer(0, 1, *grads)
    pass_on(1, by_rows[2])
    outer(0, 2, *grads)
    add_up(0, 0)
    beside(1)
    outer(0, 3, *grads)
    add_up(0, 1)
    z = jnp.zeros((members * cap, hidden), F32)
    for c in by_rows:
        z = z + inner(1, c)
    add_up(0, 2)
    grads = middle(1, all_z(1, z))
    for c in range(last[1]):
        outer(1, c, *grads)
        if c == 1:
            for d in range(3, last[0]):
                add_up(0, d)
    for c in range(last[0]):
        finish(0, c)
        add_up(1, c)
    for c in range(last[0], last[1]):
        add_up(1, c)
    for c in range(last[1]):
        finish(1, c)
    for copy in sent:
        copy.wait_send()
    for copy in written:
        copy.wait()


def per_device(pending, routes, probs, saved_gate, saved_up, w_gate, w_up, w_down, w_router):
    sections, members = lax.axis_size("section"), lax.axis_size("expert")
    experts = w_router.shape[2]
    group = members // experts
    tokens, width = pending.shape[2], pending.shape[3]
    cap = tokens // experts
    hidden = w_gate.shape[2]
    chunks, pieces = len(IN_CUT), max(len(cut) for cut in OUT_CUT)
    split = sum(IN_CUT[:SHARED]) * (width // sum(IN_CUT))
    dma, vmem = pltpu.SemaphoreType.DMA, pltpu.VMEM
    any_spec = pl.BlockSpec(memory_space=pl.ANY)
    scratch = [
        vmem((2, tokens), jnp.int32),
        vmem((2, tokens), BF16),
        vmem((2, members, cap, hidden), BF16),
        vmem((2, members, cap, hidden), BF16),
        vmem((experts, width), F32),
        vmem((2, tokens, width), BF16),
        vmem((width, 2 * hidden), BF16),
        vmem((hidden, width - split), BF16),
        vmem((group, hidden, split), BF16),
        vmem((2, group, tokens, hidden), F32),
        vmem((2, group, tokens, hidden), F32),
        vmem((2, experts, cap, width), BF16),
        vmem((2, experts, group, cap, width), BF16),
        vmem((experts, 2, cap, 128), BF16),
        vmem((members, 2, cap, 128), BF16),
        vmem((2, experts, group, cap, width), BF16),
        vmem((2, max(group - 1, 1), experts, cap, width), BF16),
        vmem((2, experts, cap, width), BF16),
        vmem((2, experts, cap, width), BF16),
        vmem((2, tokens, width), BF16),
        vmem((2, tokens, width), BF16),
        dma((2,)),
        dma((4,)),
        dma((5,)),
        dma((2, pieces)),
        dma((2, chunks)), dma((2, chunks)),
        dma((members,)), dma((members,)),
        dma((2, chunks, experts)), dma((2, chunks, experts)),
        dma((2, chunks, experts, group)), dma((2, chunks, experts, group)),
        dma((chunks, group)), dma((chunks, group)),
        dma((2, group)), dma((2, group)),
        dma((2, pieces, group)), dma((2, pieces, group)),
        dma((2, pieces, experts)), dma((2, pieces, experts)),
    ]
    room = sum(
        int(np.prod(s.shape)) * s.dtype.itemsize for s in scratch if s.memory_space == pltpu.VMEM)
    result = pl.pallas_call(
        functools.partial(layer_kernel, sections, experts, group),
        out_shape=jax.ShapeDtypeStruct((2, tokens, width), BF16),
        in_specs=[pl.BlockSpec(memory_space=pltpu.HBM)] * 9,
        out_specs=any_spec,
        scratch_shapes=scratch,
        compiler_params=pltpu.CompilerParams(
            collective_id=0, has_side_effects=True, vmem_limit_bytes=room + (8 << 20)),
        cost_estimate=pl.CostEstimate(
            flops=12 * members * cap * hidden * width, bytes_accessed=8 << 20, transcendentals=0),
    )(*[pltpu.with_memory_space_constraint(value, pltpu.HBM) for value in (
        pending[:, 0], routes[:, 0, :, 0], probs[:, 0], saved_gate[:, 0, 0], saved_up[:, 0, 0],
        w_gate[0], w_up[0], w_down[0], jnp.transpose(w_router[0]),
    )])
    return result[:, None]


def solution(mesh):
    in_specs = (
        P(None, "section", "expert", None),
        P(None, "section", "expert", None),
        P(None, "section", "expert"),
        P(None, "section", "expert", None, None, None),
        P(None, "section", "expert", None, None, None),
        P("section", None, "expert"),
        P("section", None, "expert"),
        P("section", "expert", None),
        P("section", None, None),
    )
    out_specs = P(None, "section", "expert", None)
    return jax.shard_map(
        per_device, mesh=mesh, in_specs=in_specs, out_specs=out_specs, check_vma=False
    )
```
